128 devices in a mesh: band: 8 (over x, y_lo), dom: 16 (over z, y_hi, core).
Axes of the slice: x: 4, y: 4 (y_hi: 2, y_lo: 2; y = y_hi * 2 + y_lo), z: 4, core: 2. Of those that a mesh axis runs over, the one named last changes fastest.
Arguments:
- occ_orb: bfloat16 [32, 98304], P('band', 'dom'), may hold values from -6 to 6
- vir_orb: bfloat16 [16, 98304], P('band', 'dom'), may hold values from -6 to 6
- pair_list: int32 [2, 512], replicated, may hold values from 0 to 31, as said below
- quad_weight: float32 [98304], P('dom'), may hold values from 0.3 to 27, as said below
- cell_coef: float32 [1536], P('dom'), may hold values from 1 to 10
- connect: int32 [125, 1536], P(None, 'dom'), may hold values from 0 to 6143, as said below
- face_map: int32 [2, 12288], P(None, 'dom'), may hold values from 0 to 6143, as said below
- element_matrix: float32 [125, 125], replicated, may hold values from -0.008 to 1.5, as said below
Outputs:
- potential: float32 [512, 98304], P('band', 'dom')
- coupling: float32 [512, 512], P('band', 'dom')
The draws below stay inside these ranges and needn't reach their ends.
Inputs may be any that keep to these rules, and one draw needn't show every extreme that they name: `pair_list`: row 0 holds occupied orbitals, row 1 virtual ones below 16; every combination of an occupied and a virtual orbital appears exactly once. `connect`: numbers of nodes of the cell's own subdomain (the cells of subdomain d are columns d * 96 to (d + 1) * 96 - 1); every node of a subdomain belongs to some cell. `face_map`: subdomain d owns columns d * 768 to (d + 1) * 768 - 1; its 1536 numbers are distinct; entry k of row 1 of subdomain d and entry k of row 0 of subdomain d + 1 are copies of the same node. `quad_weight`: positive. `element_matrix`: symmetric; each diagonal entry exceeds the sum of the magnitudes of the other entries of its row.
All inputs are finite; a program needn't handle non-finite values.
Results may differ from the reference program's by a relative error of at most 0.00066.
Values may be sent and summed in bfloat16 or wider, within the bound.
A program may use at most 128 MiB of HBM per device.

```python
import math
import jax
import jax.numpy as jnp
from jax import lax

OCC = 32
VIR = 16
PAIRS = 512
NPC = 125
ITERS = 3
NODE_DEV = 6144
CELL_DEV = 96
FACE = 768
NODES = 98304
CELLS = 1536


def draw_pair_list(key, part):
    key = jax.random.fold_in(key, 23)
    ordering = jax.random.permutation(key, PAIRS)
    return jnp.stack([ordering // VIR, ordering % VIR]).astype(jnp.int32)


def draw_quad_weight(key, part):
    key = jax.random.fold_in(key, 17)
    position = jnp.arange(NODES, dtype=jnp.float32) / float(NODES - 1)
    base_value = jnp.exp(jax.random.uniform(key, (NODES,), jnp.float32, jnp.log(0.3), jnp.log(3.0)))
    trend = 1.0 + 2.0 * position
    return base_value * trend


def draw_connect(key, part):
    key = jax.random.fold_in(key, 11)
    first_key, second_key, third_key = jax.random.split(key, 3)
    dom_count = CELLS // CELL_DEV
    cell_local = jnp.arange(CELLS, dtype=jnp.int32) % CELL_DEV
    owned = 64 * cell_local[None, :] + jnp.arange(64, dtype=jnp.int32)[:, None]
    hop_count = jax.random.randint(first_key, (NPC - 64, CELLS), 1, 3)
    slot_pick = jax.random.randint(second_key, (NPC - 64, CELLS), 0, 64)
    others = 64 * ((cell_local[None, :] + hop_count) % CELL_DEV) + slot_pick
    layout = jnp.concatenate([owned, others], axis=0).astype(jnp.int32)

    def shuffle_nodes(one_key):
        return jax.random.permutation(one_key, NODE_DEV).astype(jnp.int32)
    relabel = jax.vmap(shuffle_nodes)(jax.random.split(third_key, dom_count))
    cell_dom = jnp.arange(CELLS, dtype=jnp.int32) // CELL_DEV
    return relabel[cell_dom[None, :], layout].astype(jnp.int32)


def draw_face_map(key, part):
    key = jax.random.fold_in(key, 13)
    dom_count = NODES // NODE_DEV

    def one_domain(number):
        first_key, second_key = jax.random.split(jax.random.fold_in(key, number))
        middle = 1 + jax.random.permutation(first_key, NODE_DEV - 2)[:2 * FACE - 2]
        listed = jnp.concatenate([jnp.array([0, NODE_DEV - 1], jnp.int32), middle.astype(jnp.int32)])
        shuffled = listed[jax.random.permutation(second_key, 2 * FACE)]
        return shuffled.reshape(2, FACE)
    blocks = jax.vmap(one_domain)(jnp.arange(dom_count))
    return jnp.transpose(blocks, (1, 0, 2)).reshape(2, dom_count * FACE).astype(jnp.int32)


def draw_element_matrix(key, part):
    key = jax.random.fold_in(key, 19)
    first_key, second_key = jax.random.split(key)
    raw_values = jax.random.uniform(first_key, (NPC, NPC), jnp.float32, -1.0, 1.0)
    off_part = (raw_values + raw_values.T) * (0.5 / NPC)
    identity = jnp.eye(NPC, dtype=jnp.float32)
    diag_values = jax.random.uniform(second_key, (NPC,), jnp.float32, 1.0, 1.5)
    return off_part * (1.0 - identity) + identity * diag_values[None, :]


def levels(key, shape, pieces, low, high):
    factor_of = 1.0
    for dim, parts in pieces:
        draws = jax.random.uniform(jax.random.fold_in(jax.random.fold_in(key, 6), dim), (parts,), jnp.float32, low / len(pieces), high / len(pieces))
        factor_of = factor_of * jnp.repeat(jnp.exp(draws), shape[dim] // parts).reshape((-1,) + (1,) * (len(shape) - 1 - dim))
    return factor_of


def noise(rng, shape, deviation, limit, cuts=(), held_as=jnp.bfloat16):
    level = levels(rng, shape, cuts, -0.22, 0.18) if cuts else 1.0
    entries = jax.random.normal(rng, shape, jnp.float32) * deviation * level
    return jnp.minimum(jnp.maximum(entries, -limit), limit).astype(held_as)


def setup_inputs(seed: int = 0) -> dict:
    streams_of = jax.random.split(jax.random.key(seed), 9)
    return {
        "occ_orb": noise(streams_of[0], (OCC, NODES), 1.0, 6.0, ((0, 8), (1, 16))),
        "vir_orb": noise(streams_of[1], (VIR, NODES), 1.0, 6.0, ((0, 8), (1, 16))),
        "pair_list": draw_pair_list(jax.random.fold_in(streams_of[8], 71), 0),
        "quad_weight": draw_quad_weight(jax.random.fold_in(streams_of[8], 71), 0),
        "cell_coef": jnp.clip(jnp.exp(math.log(10.0) - 2.3025851 * jax.random.uniform(streams_of[4], (CELLS,), jnp.float32) ** levels(streams_of[4], (CELLS,), ((0, 16),), -0.2, 0.2)), 1.0, 10.0),
        "connect": draw_connect(jax.random.fold_in(streams_of[8], 71), 0),
        "face_map": draw_face_map(jax.random.fold_in(streams_of[8], 71), 0),
        "element_matrix": draw_element_matrix(jax.random.fold_in(streams_of[8], 71), 0),
    }


def faces_global(face_map):
    dom_count = NODES // NODE_DEV
    offsets = (jnp.arange(dom_count, dtype=jnp.int32) * NODE_DEV)[:, None]
    lower_face = face_map[0].reshape(dom_count, FACE) + offsets
    upper_face = face_map[1].reshape(dom_count, FACE) + offsets
    return lower_face[1:].reshape(-1), upper_face[:-1].reshape(-1)


def assemble(local_sum, lower_index, upper_index):
    from_below = local_sum[:, upper_index]
    from_above = local_sum[:, lower_index]
    return local_sum.at[:, lower_index].add(from_below).at[:, upper_index].add(from_above)


def operate(field_values, conn_global, cell_coef, element_matrix, lower_index, upper_index):
    cell_values = field_values[:, conn_global]
    cell_product = jnp.einsum("ij,bjc->bic", element_matrix, cell_values, precision=lax.Precision.HIGHEST) * cell_coef
    local_sum = jnp.zeros_like(field_values).at[:, conn_global].add(cell_product)
    return assemble(local_sum, lower_index, upper_index)


def reference(occ_orb, vir_orb, pair_list, quad_weight, cell_coef, connect, face_map, element_matrix):
    lower_index, upper_index = faces_global(face_map)
    conn_global = connect + (jnp.arange(CELLS, dtype=jnp.int32) // CELL_DEV * NODE_DEV)[None, :]
    node_share = jnp.ones((NODES,), jnp.float32).at[lower_index].set(0.5).at[upper_index].set(0.5)
    block_count = PAIRS // 32
    pair_blocks = jnp.transpose(pair_list.reshape(2, block_count, 32), (1, 0, 2))

    def solve_block(block_pairs):
        density = occ_orb[block_pairs[0]].astype(jnp.float32) * vir_orb[block_pairs[1]].astype(jnp.float32)
        local_rhs = density * quad_weight
        right_side = assemble(local_rhs, lower_index, upper_index)
        solution = jnp.zeros_like(right_side)
        residual = right_side
        direction = right_side
        norm_now = jnp.sum(node_share * residual * residual, axis=1)
        for iteration in range(ITERS):
            applied = operate(direction, conn_global, cell_coef, element_matrix, lower_index, upper_index)
            curv_total = jnp.sum(node_share * direction * applied, axis=1)
            step_size = norm_now / curv_total
            solution = solution + step_size[:, None] * direction
            residual = residual - step_size[:, None] * applied
            norm_next = jnp.sum(node_share * residual * residual, axis=1)
            direction = residual + (norm_next / norm_now)[:, None] * direction
            norm_now = norm_next
        return solution, local_rhs.astype(jnp.bfloat16)

    potential, weighted = lax.map(solve_block, pair_blocks)
    potential = potential.reshape(PAIRS, NODES)
    weighted = weighted.reshape(PAIRS, NODES)
    rounded_potential = potential.astype(jnp.bfloat16)
    coupling = lax.dot_general(weighted, rounded_potential, (((1,), (1,)), ((), ())), preferred_element_type=jnp.float32)
    return potential, coupling / float(NODES)
```

```python
import jax
import jax.numpy as jnp
from jax import lax
from jax.experimental import pallas as pl
from jax.experimental.pallas import tpu as pltpu
from jax.sharding import PartitionSpec as P

NODES = 6144
TILES = 48
CELLS = 96
NPC = 125
FACE = 768
BAND = 8
DOM = 16
PAIRS = 512
OWN = 64
ENTRY_TILES = 47
STEPS = ENTRY_TILES + TILES - 1
F32 = jnp.float32
BF16 = jnp.bfloat16
I32 = jnp.int32
MESH = pl.DeviceIdType.MESH


def iota(shape, dim):
    return lax.broadcasted_iota(I32, shape, dim)


def contract(first, second, dims):
    return lax.dot_general(first, second, (dims, ((), ())), preferred_element_type=F32)


def index_kernel(conn_ref, face_ref, key_ref, node_ref, new_ref, old_ref):
    rows48 = iota((TILES, 128), 0)
    rows128 = iota((128, 128), 0)
    lane_row = iota((1, 128), 1)

    def table(numbers, base, hit, low):
        high_hot = jnp.where(lax.shift_right_logical(numbers, 7) == rows48, 1.0, 0.0).astype(BF16)
        same = (numbers & 127) == rows128
        low_hot = jnp.where(same, 1.0, 0.0).astype(BF16)
        low_value = jnp.where(same, lane_row, 0).astype(F32).astype(BF16)
        hits = contract(high_hot, low_hot, ((1,), (1,)))
        values = contract(high_hot, low_value, ((1,), (1,)))
        return hit + hits, low + values + base * hits

    shared = jnp.zeros((TILES, 128), F32)
    face_id = jnp.zeros((TILES, 128), F32)
    for j in range(2 * FACE // 128):
        shared, face_id = table(face_ref[j : j + 1, :], 128.0 * j, shared, face_id)
    inner = 1.0 - shared
    inner16 = inner.astype(BF16)
    before = jnp.where(iota((128, 128), 0) < iota((128, 128), 1), 1.0, 0.0).astype(BF16)
    above = jnp.where(iota((TILES, TILES), 1) < iota((TILES, TILES), 0), 1.0, 0.0).astype(BF16)
    in_row = contract(inner16, before, ((1,), (0,)))
    rows_above = jnp.sum(contract(above, inner16, ((1,), (0,))), axis=1, keepdims=True)
    number = jnp.where(shared > 0.5, face_id, in_row + rows_above + 2.0 * FACE)
    new_ref[...] = number.astype(I32)

    def invert(j, carry):
        hit, low = carry
        base = (128 * j).astype(F32)
        return table(new_ref[pl.ds(j, 1), :], base, hit, low)

    zero = jnp.zeros((TILES, 128), F32)
    _, old = lax.fori_loop(0, TILES, invert, (zero, zero))
    old_ref[...] = old.astype(I32)

    number_int = number.astype(I32)
    high_part = lax.shift_right_logical(number_int, 7).astype(F32)
    low_part = (number_int & 127).astype(F32)
    parts = jnp.concatenate([high_part, low_part], axis=1).T.astype(BF16)

    def look_up(group, _):
        found = []
        for u in range(8):
            nodes = conn_ref[pl.ds(group * 8 + u, 1), :]
            hot = jnp.where(lax.shift_right_logical(nodes, 7) == rows48, 1.0, 0.0).astype(BF16)
            both = contract(parts, hot, ((1,), (0,)))
            value = 128.0 * both[:128] + both[128:]
            same = (nodes & 127) == rows128
            found.append(jnp.sum(jnp.where(same, value, 0.0), axis=0, keepdims=True))
        ids = jnp.concatenate(found, axis=0).astype(I32)
        lanes = iota((8, 128), 1)
        code = (iota((8, 128), 0) + group * 8) * 128 + lanes
        real = lanes < NPC
        at = pl.ds(pl.multiple_of(group * 8, 8), 8)
        key_ref[at, :] = jnp.where(real, ids, NODES) * 16384 + code
        node_ref[at, :] = jnp.where(real, ids, 0)
        return 0

    lax.fori_loop(0, CELLS // 8, look_up, 0)


def build_index(connect, face_map):
    conn = jnp.pad(connect.T, ((0, 0), (0, 128 - NPC)))
    face = face_map.reshape(2 * FACE // 128, 128)
    vmem = pl.BlockSpec(memory_space=pltpu.VMEM)
    shape = jax.ShapeDtypeStruct
    key, node, new, old = pl.pallas_call(
        index_kernel,
        out_shape=[
            shape((CELLS, 128), I32),
            shape((CELLS, 128), I32),
            shape((TILES, 128), I32),
            shape((TILES, 128), I32),
        ],
        in_specs=[vmem, vmem],
        out_specs=[vmem] * 4,
        name="index",
    )(conn, face)
    ordered = lax.sort(key.reshape(CELLS * 128), is_stable=False)
    perm = (ordered & 16383).reshape(TILES, 256)
    sid = lax.shift_right_logical(ordered, 14).reshape(TILES, 256)
    first = lax.shift_right_logical(ordered.reshape(TILES, 256)[:ENTRY_TILES, 0], 21)
    places = jnp.arange(TILES, dtype=I32)
    last = jnp.sum((first[None, :] <= places[:, None]).astype(I32), axis=1) - 1 + places
    steps = jnp.arange(128, dtype=I32)
    node_tile = jnp.sum((last[None, :] < steps[:, None]).astype(I32), axis=1)
    previous = jnp.sum((last[None, :] < steps[:, None] - 1).astype(I32), axis=1)
    keep = ((node_tile == previous) & (steps > 0)).astype(F32)
    walk = jnp.stack([steps - node_tile, node_tile, jnp.pad(last, (0, 128 - TILES))])
    return node, perm, sid, walk, keep, new, old


def main_kernel(
    node_s, perm_s, walk_s, keep_s, new_s, old_s, coef_s,
    sid_v, orb_v, quad_v, pairs_v, elem_v,
    pot_out, coup_out,
    orb_all, orbf, pick3, pick_occ, pick_vir, elem2,
    rhs, r0, r1, r2, im0, split, y_buf, x_buf, p_buf, w_buf, ga, gb, zf, pot16, c_acc,
    face_send, face_recv, dot_send, dot_recv, c_send, c_recv,
    orb_ss, orb_rs, face_ss, face_rs, dot_ss, dot_rs, c_ss, c_rs,
):
    dom = lax.axis_index("dom")
    band = lax.axis_index("band")
    half_dom = lax.div(dom, 2)
    low_half = iota((128, 128), 1) < 64

    def swap(value):
        return pltpu.roll(value, 64, 1)

    def halves(value):
        high = value.astype(BF16).astype(F32)
        return jnp.where(low_half, high, value - high)

    def tile(j):
        return pl.ds(pl.multiple_of(j * 128, 128), 128)

    def fold(value):
        return jnp.sum(value.reshape(16, 8, 128), axis=0)

    barrier = pltpu.get_barrier_semaphore()
    for off in range(1, BAND):
        pl.semaphore_signal(
            barrier, 1, device_id={"band": lax.rem(band + off, BAND)}, device_id_type=MESH
        )
    for off in range(1, DOM):
        pl.semaphore_signal(
            barrier, 1, device_id={"dom": lax.rem(dom + off, DOM)}, device_id_type=MESH
        )
    mine = half_dom == band
    for off in range(DOM):
        source = lax.rem(dom + off, DOM)

        @pl.when(jnp.logical_not(jnp.logical_and(mine, source == dom)))
        def _():
            pl.semaphore_signal(
                barrier, 1, device_id={"band": half_dom, "dom": source}, device_id_type=MESH
            )

    occ_of = pairs_v[0:1, :]
    vir_of = pairs_v[1:2, :]
    orbital = iota((64, PAIRS), 0)
    occ_hot = jnp.where(orbital == occ_of, 1.0, 0.0)
    vir_hot = jnp.where(orbital == vir_of + 32, 1.0, 0.0)
    pick_occ[...] = occ_hot.T.astype(BF16)
    pick_vir[...] = vir_hot.T.astype(BF16)
    own = (iota((PAIRS, 128), 1) & 63) + band * OWN == iota((PAIRS, 128), 0)
    own = jnp.where(own, 1.0, 0.0).astype(BF16)
    pick3[:, 0:128] = contract(occ_hot.astype(BF16), own, ((1,), (0,))).astype(BF16)
    pick3[:, 128:256] = contract(vir_hot.astype(BF16), own, ((1,), (0,))).astype(BF16)
    weight_row = iota((64, 128), 0)
    weight_row = jnp.logical_and(weight_row >= 48, weight_row < 51)
    pick3[:, 256:384] = jnp.where(weight_row, 1.0, 0.0).astype(BF16)
    elem = elem_v[...]
    elem_high = elem.astype(BF16)
    elem2[:, 0:128] = elem_high
    elem2[:, 128:256] = (elem - elem_high.astype(F32)).astype(BF16)
    quad = quad_v[...]
    quad_high = quad.astype(BF16).astype(F32)
    quad_rest = quad - quad_high
    quad_mid = quad_rest.astype(BF16).astype(F32)
    orbf[48 * TILES : 49 * TILES, :] = quad_high
    orbf[49 * TILES : 50 * TILES, :] = quad_mid
    orbf[50 * TILES : 51 * TILES, :] = quad_rest - quad_mid
    orbf[51 * TILES : 64 * TILES, :] = jnp.zeros((13 * TILES, 128), F32)
    for buf in (ga, gb):
        buf[120:128, :] = jnp.zeros((8, 128), F32)
        buf[248:256, :] = jnp.zeros((8, 128), F32)

    @pl.when(mine)
    def _():
        pl.semaphore_wait(barrier, BAND - 1 + DOM - 1 + DOM - 1)

    @pl.when(jnp.logical_not(mine))
    def _():
        pl.semaphore_wait(barrier, BAND - 1 + DOM - 1 + DOM)

    orb_copies = []
    for off in range(1, BAND):
        copy = pltpu.make_async_remote_copy(
            src_ref=orb_v,
            dst_ref=orb_all.at[band],
            send_sem=orb_ss.at[off],
            recv_sem=orb_rs.at[band],
            device_id={"band": lax.rem(band + off, BAND)},
            device_id_type=MESH,
        )
        copy.start()
        orb_copies.append(copy)
    orb_all[band] = orb_v[...]
    for off in range(1, BAND):
        source = lax.rem(band + off, BAND)
        pltpu.make_async_remote_copy(
            src_ref=orb_v,
            dst_ref=orb_all.at[source],
            send_sem=orb_ss.at[off],
            recv_sem=orb_rs.at[source],
            device_id={"band": source},
            device_id_type=MESH,
        ).wait_recv()
    for b in range(BAND):
        for o in range(4):
            orbf[(4 * b + o) * TILES : (4 * b + o + 1) * TILES, :] = orb_all[b, o].astype(F32)
        for o in range(2):
            at = 32 + 2 * b + o
            orbf[at * TILES : (at + 1) * TILES, :] = orb_all[b, 4 + o].astype(F32)

    def form(j, _):
        orbs = orbf[pl.ds(j, 64, stride=TILES), :].astype(BF16)
        rows = contract(orbs, pick3[...], ((0,), (0,)))
        rhs[tile(j), :] = rows[:, 0:128] * rows[:, 128:256] * rows[:, 256:384]
        return 0

    lax.fori_loop(0, TILES, form, 0)

    def renumber(j, _):
        base = pl.multiple_of(j * 128, 128)
        for u in range(128):
            r0[pl.ds(base + u, 1), :] = rhs[pl.ds(old_s[j, u], 1), :]
        return 0

    has_below = dom > 0
    has_above = dom < DOM - 1

    def face_copy(rnd, side, target):
        return pltpu.make_async_remote_copy(
            src_ref=face_send.at[rnd, 1 - side],
            dst_ref=face_recv.at[rnd, side],
            send_sem=face_ss.at[rnd, side],
            recv_sem=face_rs.at[rnd, side],
            device_id={"dom": target},
            device_id_type=MESH,
        )

    def send_faces(rnd):
        @pl.when(has_above)
        def _():
            face_copy(rnd, 0, dom + 1).start()

        @pl.when(has_below)
        def _():
            face_copy(rnd, 1, dom - 1).start()

    def add_faces(rnd, field):
        @pl.when(has_below)
        def _():
            face_copy(rnd, 0, dom - 1).wait_recv()

            def body(j, _):
                got = face_recv[rnd, 0, tile(j), :].astype(F32)
                field[tile(j), :] += got + swap(got)
                return 0

            lax.fori_loop(0, 6, body, 0)

        @pl.when(has_above)
        def _():
            face_copy(rnd, 1, dom + 1).wait_recv()

            def body(j, _):
                got = face_recv[rnd, 1, tile(j), :].astype(F32)
                field[tile(j + 6), :] += got + swap(got)
                return 0

            lax.fori_loop(0, 6, body, 0)

        @pl.when(has_above)
        def _():
            face_copy(rnd, 0, dom + 1).wait_send()

        @pl.when(has_below)
        def _():
            face_copy(rnd, 1, dom - 1).wait_send()

    def pack_faces(rnd, field):
        def body(j, _):
            for side in range(2):
                value = field[tile(j + 6 * side), :]
                face_send[rnd, side, tile(j), :] = halves(value).astype(BF16)
            return 0

        lax.fori_loop(0, 6, body, 0)

    lax.fori_loop(0, 12, renumber, 0)
    pack_faces(0, r0)
    send_faces(0)
    lax.fori_loop(12, TILES, renumber, 0)
    add_faces(0, r0)

    lower_share = jnp.where(has_below, 0.5, 1.0).astype(F32)
    upper_share = jnp.where(has_above, 0.5, 1.0).astype(F32)
    zero_acc = jnp.zeros((8, 128), F32)

    ranges = ((0, 6, lower_share), (6, 12, upper_share), (12, TILES, 1.0))
    rr_part = zero_acc
    for start, stop, share in ranges:

        def start_split(j, acc):
            value = r0[tile(j), :]
            split[tile(j), :] = halves(value)
            return acc + fold(value * value)

        rr_part = rr_part + share * lax.fori_loop(start, stop, start_split, zero_acc)
    rd_part = zero_acc

    def gather_pair(i, buf):
        for h in range(2):
            for u in range(NPC):
                buf[pl.ds(128 * h + u, 1), :] = split[pl.ds(node_s[2 * i + h, u], 1), :]

    def cell_pair(i, buf, acc, keep_rows):
        first = buf[0:128, :]
        second = buf[128:256, :]
        both = jnp.concatenate([first.astype(BF16), second.astype(BF16)], axis=1)
        product = contract(elem2[...], jnp.concatenate([both, both], axis=0), ((1,), (0,)))
        for h, held in ((0, first), (1, second)):
            rows = product[:, 128 * h : 128 * h + 128]
            rows = (rows + swap(rows)) * coef_s[2 * i + h]
            acc = acc + fold(held * rows)
            if keep_rows:
                y_buf[tile(2 * i + h), :] = halves(rows)
        return acc

    def cells(keep_rows):
        gather_pair(0, ga)

        def body(i, acc):
            gather_pair(2 * i + 1, gb)
            acc = cell_pair(2 * i, ga, acc, keep_rows)
            gather_pair(2 * i + 2, ga)
            return cell_pair(2 * i + 1, gb, acc, keep_rows)

        acc = lax.fori_loop(0, CELLS // 4 - 1, body, zero_acc)
        gather_pair(CELLS // 2 - 1, gb)
        acc = cell_pair(CELLS // 2 - 2, ga, acc, keep_rows)
        return cell_pair(CELLS // 2 - 1, gb, acc, keep_rows)

    def one_row(value):
        return jnp.sum(value, axis=0, keepdims=True)

    def send_dots(rnd, rows):
        packed = jnp.concatenate(rows + [jnp.zeros((8 - len(rows), 128), F32)], axis=0)
        dot_send[rnd] = packed
        dot_recv[rnd, dom] = packed
        for off in range(1, DOM):
            pltpu.make_async_remote_copy(
                src_ref=dot_send.at[rnd],
                dst_ref=dot_recv.at[rnd, dom],
                send_sem=dot_ss.at[rnd, off],
                recv_sem=dot_rs.at[rnd, dom],
                device_id={"dom": lax.rem(dom + off, DOM)},
                device_id_type=MESH,
            ).start()

    def sum_dots(rnd):
        for off in range(1, DOM):
            source = lax.rem(dom + off, DOM)
            copy = pltpu.make_async_remote_copy(
                src_ref=dot_send.at[rnd],
                dst_ref=dot_recv.at[rnd, source],
                send_sem=dot_ss.at[rnd, off],
                recv_sem=dot_rs.at[rnd, source],
                device_id={"dom": source},
                device_id_type=MESH,
            )
            copy.wait_recv()
            copy.wait_send()
        total = jnp.sum(dot_recv[rnd], axis=0)
        return [total[k : k + 1, :] for k in range(3)]

    def gather_entries(t, _):
        for u in range(256):
            x_buf[t, pl.ds(u, 1), :] = y_buf[pl.ds(perm_s[t, u], 1), :]
        return 0

    node_rows = iota((128, 256), 0)

    def sum_entries(p, acc):
        t = walk_s[0, p]
        j = walk_s[1, p]
        keep = keep_s[p]
        ids = sid_v[pl.ds(t, 1), :] - j * 128
        hot = jnp.where(ids == node_rows, 1.0, 0.0).astype(BF16)
        rows = x_buf[t].astype(BF16)
        acc = acc * keep + contract(hot, rows, ((1,), (0,)))
        p_buf[p] = acc
        return acc

    def take(j):
        value = p_buf[walk_s[2, j]]
        return value + swap(value)

    def weigh(j, _):
        for u in range(2):
            orbs = orbf[pl.ds(2 * j + u, 64, stride=TILES), :].astype(BF16)
            occ = contract(pick_occ[...], orbs, ((1,), (0,)))
            vir = contract(pick_vir[...], orbs, ((1,), (0,)))
            at = pl.ds(pl.multiple_of((2 * j + u) * 128, 128), 128)
            w_buf[:, at] = (occ * vir * quad_v[pl.ds(2 * j + u, 1), :]).astype(BF16)
        return 0

    old_rr = old_den = beta = None
    fields = (r0, r1, r2)
    steps = []
    for it in range(2):
        now, later = fields[it], fields[it + 1]
        quad_part = one_row(cells(True))
        send_dots(it + 1, [one_row(rr_part), one_row(rd_part), quad_part + swap(quad_part)])
        lax.fori_loop(0, ENTRY_TILES, gather_entries, 0)
        lax.fori_loop(0, STEPS, sum_entries, jnp.zeros((128, 128), F32))

        def set_faces(j, _):
            value = take(j)
            zf[tile(j), :] = value
            return 0

        lax.fori_loop(0, 12, set_faces, 0)
        pack_faces(it + 1, zf)
        send_faces(it + 1)
        lax.fori_loop(12 * it, 12 * it + 12, weigh, 0)
        rr, rd, quad_form = sum_dots(it + 1)
        if it == 0:
            den = quad_form
        else:
            beta = rr / old_rr
            den = quad_form + 2.0 * beta * rd + beta * beta * old_den
        alpha = rr / den
        steps.append((alpha, beta))

        def advance(j, value, accs, it=it, now=now, later=later, alpha=alpha, beta=beta):
            image = value
            if it == 0:
                im0[tile(j), :] = image
            else:
                image = image + beta * im0[tile(j), :]
            new = now[tile(j), :] - alpha * image
            later[tile(j), :] = new
            split[tile(j), :] = halves(new)
            return accs[0] + fold(new * new), accs[1] + fold(new * image)

        none = (zero_acc, zero_acc)
        rr_part, rd_part = lax.fori_loop(12, TILES, lambda j, a: advance(j, take(j), a), none)
        add_faces(it + 1, zf)
        for start, stop, share in ranges[:2]:
            more = lax.fori_loop(start, stop, lambda j, a: advance(j, zf[tile(j), :], a), none)
            rr_part = rr_part + share * more[0]
            rd_part = rd_part + share * more[1]
        old_rr, old_den = rr, den

    quad_part = one_row(cells(False))
    send_dots(3, [one_row(rr_part), one_row(rd_part), quad_part + swap(quad_part)])
    rr, rd, quad_form = sum_dots(3)
    last_beta = rr / old_rr
    den = quad_form + 2.0 * last_beta * rd + last_beta * last_beta * old_den
    scale2 = rr / den
    scale1 = steps[1][0] + scale2 * last_beta
    scale0 = steps[0][0] + scale1 * steps[1][1]

    def combine(j, _):
        at = tile(j)
        split[at, :] = scale0 * r0[at, :] + scale1 * r1[at, :] + scale2 * r2[at, :]
        return 0

    lax.fori_loop(0, TILES, combine, 0)

    def restore(j, _):
        for u in range(128):
            ga[pl.ds(u, 1), :] = split[pl.ds(new_s[j, u], 1), :]
        value = ga[0:128, :]
        pot16[tile(j), :] = value.astype(BF16)
        pot_out[:, tile(j)] = value.T[0:OWN, :]
        return 0

    lax.fori_loop(0, TILES, restore, 0)

    c_acc[...] = jnp.zeros((PAIRS, 128), F32)

    def couple(k, _):
        at = pl.ds(pl.multiple_of(k * 512, 512), 512)
        c_acc[...] += contract(w_buf[:, at], pot16[at, :], ((1,), (0,)))
        return 0

    lax.fori_loop(0, NODES // 512, couple, 0)

    def c_copy(piece, slot, device):
        return pltpu.make_async_remote_copy(
            src_ref=c_send.at[piece],
            dst_ref=c_recv.at[slot],
            send_sem=c_ss.at[piece],
            recv_sem=c_rs.at[slot],
            device_id=device,
            device_id_type=MESH,
        )

    for b in range(BAND):
        block = c_acc[OWN * b : OWN * b + OWN, :]
        turned = jnp.concatenate([block, block], axis=0).T
        for h in range(2):
            piece = 2 * b + h
            c_send[piece] = turned[32 * h : 32 * h + 32, :]
            to_self = jnp.logical_and(band == b, dom == 2 * band + h)

            @pl.when(jnp.logical_not(to_self))
            def _(b=b, h=h, piece=piece):
                c_copy(piece, dom, {"band": b, "dom": 2 * band + h}).start()

            @pl.when(to_self)
            def _(piece=piece):
                c_recv[dom] = c_send[piece]

    for off in range(DOM):
        source = lax.rem(dom + off, DOM)
        from_self = jnp.logical_and(mine, source == dom)

        @pl.when(jnp.logical_not(from_self))
        def _(source=source):
            c_copy(0, source, {"band": half_dom, "dom": source}).wait_recv()

    total = jnp.sum(c_recv[...], axis=0) * (1.0 / (NODES * DOM))
    coup_out[...] = jnp.concatenate([total] * 4, axis=0).T[0:OWN, 0:32]

    for copy in orb_copies:
        copy.wait_send()
    for b in range(BAND):
        for h in range(2):
            piece = 2 * b + h
            to_self = jnp.logical_and(band == b, dom == 2 * band + h)

            @pl.when(jnp.logical_not(to_self))
            def _(b=b, h=h, piece=piece):
                c_copy(piece, dom, {"band": b, "dom": 2 * band + h}).wait_send()


def on_device(
    occ_orb, vir_orb, pair_list, quad_weight, cell_coef, connect, face_map, element_matrix
):
    node, perm, sid, walk, keep, new, old = build_index(connect, face_map)
    orbs = jnp.concatenate([occ_orb, vir_orb], axis=0).reshape(6, TILES, 128)
    quad = quad_weight.reshape(TILES, 128)
    elem = jnp.pad(element_matrix, ((0, 128 - NPC), (0, 128 - NPC)))
    vmem = pl.BlockSpec(memory_space=pltpu.VMEM)
    smem = pl.BlockSpec(memory_space=pltpu.SMEM)
    dma = pltpu.SemaphoreType.DMA
    field = pltpu.VMEM((NODES, 128), F32)
    return pl.pallas_call(
        main_kernel,
        out_shape=(
            jax.ShapeDtypeStruct((OWN, NODES), F32),
            jax.ShapeDtypeStruct((OWN, 32), F32),
        ),
        in_specs=[smem] * 7 + [vmem] * 5,
        out_specs=(vmem, vmem),
        scratch_shapes=[
            pltpu.VMEM((BAND, 6, TILES, 128), BF16),
            pltpu.VMEM((64 * TILES, 128), F32),
            pltpu.VMEM((64, 384), BF16),
            pltpu.VMEM((PAIRS, 64), BF16),
            pltpu.VMEM((PAIRS, 64), BF16),
            pltpu.VMEM((128, 256), BF16),
            field, field, field, field, field, field,
            pltpu.VMEM((CELLS * 128, 128), F32),
            pltpu.VMEM((ENTRY_TILES, 256, 128), F32),
            pltpu.VMEM((STEPS, 128, 128), F32),
            pltpu.VMEM((PAIRS, NODES), BF16),
            pltpu.VMEM((256, 128), F32),
            pltpu.VMEM((256, 128), F32),
            pltpu.VMEM((2 * FACE, 128), F32),
            pltpu.VMEM((NODES, 128), BF16),
            pltpu.VMEM((PAIRS, 128), F32),
            pltpu.VMEM((3, 2, FACE, 128), BF16),
            pltpu.VMEM((3, 2, FACE, 128), BF16),
            pltpu.VMEM((4, 8, 128), F32),
            pltpu.VMEM((4, DOM, 8, 128), F32),
            pltpu.VMEM((DOM, 32, 128), F32),
            pltpu.VMEM((DOM, 32, 128), F32),
            dma((BAND,)),
            dma((BAND,)),
            dma((3, 2)),
            dma((3, 2)),
            dma((4, DOM)),
            dma((4, DOM)),
            dma((DOM,)),
            dma((DOM,)),
        ],
        compiler_params=pltpu.CompilerParams(
            collective_id=0, has_side_effects=True, vmem_limit_bytes=60 * 1024 * 1024
        ),
        name="solve",
    )(node, perm, walk, keep, new, old, cell_coef, sid, orbs, quad, pair_list, elem)


def solution(mesh):
    return jax.shard_map(
        on_device,
        mesh=mesh,
        in_specs=(
            P("band", "dom"),
            P("band", "dom"),
            P(),
            P("dom"),
            P("dom"),
            P(None, "dom"),
            P(None, "dom"),
            P(),
        ),
        out_specs=(P("band", "dom"), P("band", "dom")),
        check_vma=False,
    )
```

```python
import jax
import jax.numpy as jnp
from jax import lax
from jax.experimental import pallas as pl
from jax.experimental.pallas import tpu as pltpu
from jax.sharding import PartitionSpec as P

NODES = 6144
TILES = 48
CELLS = 96
NPC = 125
FACE = 768
BAND = 8
DOM = 16
PAIRS = 512
OWN = 64
ENTRY_TILES = 48
WINDOW = 5
F32 = jnp.float32
BF16 = jnp.bfloat16
I32 = jnp.int32
MESH = pl.DeviceIdType.MESH


def iota(shape, dim):
    return lax.broadcasted_iota(I32, shape, dim)


def contract(first, second, dims):
    return lax.dot_general(first, second, (dims, ((), ())), preferred_element_type=F32)


def index_kernel(conn_ref, face_ref, key_ref, node_ref, new_ref, old_ref, turn):
    rows48 = iota((TILES, 128), 0)
    rows128 = iota((128, 128), 0)
    lane_row = iota((1, 128), 1)

    def table(numbers, base, hit, low):
        high_hot = jnp.where(lax.shift_right_logical(numbers, 7) == rows48, 1.0, 0.0).astype(BF16)
        same = (numbers & 127) == rows128
        low_hot = jnp.where(same, 1.0, 0.0).astype(BF16)
        low_value = jnp.where(same, lane_row, 0).astype(F32).astype(BF16)
        hits = contract(high_hot, low_hot, ((1,), (1,)))
        values = contract(high_hot, low_value, ((1,), (1,)))
        return hit + hits, low + values + base * hits

    turn[...] = jnp.zeros((128, 128), F32)
    turn[0:NPC, 0:CELLS] = conn_ref[...].astype(F32)
    turn[...] = turn[...].T
    shared = jnp.zeros((TILES, 128), F32)
    face_id = jnp.zeros((TILES, 128), F32)
    faces = [face_ref[k : k + 1, 128 * j : 128 * j + 128] for k in range(2) for j in range(6)]
    for j in range(2 * FACE // 128):
        shared, face_id = table(faces[j], 128.0 * j, shared, face_id)
    inner = 1.0 - shared
    inner16 = inner.astype(BF16)
    before = jnp.where(iota((128, 128), 0) < iota((128, 128), 1), 1.0, 0.0).astype(BF16)
    above = jnp.where(iota((TILES, TILES), 1) < iota((TILES, TILES), 0), 1.0, 0.0).astype(BF16)
    in_row = contract(inner16, before, ((1,), (0,)))
    rows_above = jnp.sum(contract(above, inner16, ((1,), (0,))), axis=1, keepdims=True)
    number = jnp.where(shared > 0.5, face_id, in_row + rows_above + 2.0 * FACE)
    new_ref[...] = number.astype(I32)

    def invert(group, carry):
        hit, low = carry
        for u in range(8):
            base = (1024 * group + 128 * u).astype(F32)
            hit, low = table(new_ref[pl.ds(8 * group + u, 1), :], base, hit, low)
        return hit, low

    zero = jnp.zeros((TILES, 128), F32)
    _, old = lax.fori_loop(0, TILES // 8, invert, (zero, zero))
    old_ref[...] = old.astype(I32)

    number_int = number.astype(I32)
    high_part = lax.shift_right_logical(number_int, 7).astype(F32)
    low_part = (number_int & 127).astype(F32)
    parts = jnp.concatenate([high_part, low_part], axis=1).T.astype(BF16)

    def look_up(group, _):
        found = []
        for u in range(8):
            nodes = turn[pl.ds(group * 8 + u, 1), :].astype(I32)
            hot = jnp.where(lax.shift_right_logical(nodes, 7) == rows48, 1.0, 0.0).astype(BF16)
            both = contract(parts, hot, ((1,), (0,)))
            value = 128.0 * both[:128] + both[128:]
            same = (nodes & 127) == rows128
            found.append(jnp.sum(jnp.where(same, value, 0.0), axis=0, keepdims=True))
        ids = jnp.concatenate(found, axis=0).astype(I32)
        lanes = iota((8, 128), 1)
        code = (iota((8, 128), 0) + group * 8) * 128 + lanes
        real = lanes < NPC
        at = pl.ds(pl.multiple_of(group * 8, 8), 8)
        key_ref[at, :] = jnp.where(real, ids, NODES) * 16384 + code
        node_ref[at, :] = jnp.where(real, ids, 0)
        return 0

    lax.fori_loop(0, CELLS // 8, look_up, 0)


def build_index(connect, face_map):
    vmem = pl.BlockSpec(memory_space=pltpu.VMEM)
    shape = jax.ShapeDtypeStruct
    key, node, new, old = pl.pallas_call(
        index_kernel,
        out_shape=[
            shape((CELLS, 128), I32),
            shape((CELLS, 128), I32),
            shape((TILES, 128), I32),
            shape((TILES, 128), I32),
        ],
        in_specs=[vmem, vmem],
        out_specs=[vmem] * 4,
        scratch_shapes=[pltpu.VMEM((128, 128), F32)],
        name="index",
    )(connect, face_map)
    ordered = lax.sort(key.reshape(CELLS * 128), is_stable=False).reshape(CELLS, 128)
    block = lax.shift_right_logical(ordered[0:94:2, 0], 20)
    place = jnp.arange(128, dtype=I32)
    begins = block[None, :] <= place[:, None]
    last_tile = jnp.sum(begins.astype(I32), axis=1) - 1
    last_block = jnp.max(jnp.where(begins, block[None, :], 0), axis=1)
    within = jnp.clip(place - last_block, 0, WINDOW - 1)
    move = jnp.clip(block - jnp.concatenate([block[:1], block[:-1]]), 0, WINDOW - 1)
    walk = jnp.stack(
        [jnp.pad(block, (0, 81)), jnp.pad(move, (0, 81)), jnp.clip(last_tile, 0, 46), within]
    )
    return node, ordered, ordered & 16383, walk, new, old


def main_kernel(
    walk_s, new_s, old_s, coef_s,
    node_v, perm_v, ordered_v, orb_v, quad_v, pairs_v, elem_v,
    pot_out, coup_out,
    orb_all, orbf, pick3, pick_occ, pick_vir, elem2,
    rhs, r0, r1, r2, im0, split, y_buf, gx, window, sums, w_buf, ga, zf, pot16, c_acc, sid_v, index_a, index_b,
    face_send, face_recv, dot_send, dot_recv, c_send, c_recv,
    orb_ss, orb_rs, face_ss, face_rs, dot_ss, dot_rs, c_ss, c_rs, index_sem,
):
    dom = lax.axis_index("dom")
    band = lax.axis_index("band")
    half_dom = lax.div(dom, 2)
    low_half = iota((128, 128), 1) < 64

    def swap(value):
        return pltpu.roll(value, 64, 1)

    def halves(value):
        high = value.astype(BF16).astype(F32)
        return jnp.where(low_half, high, value - high)

    def tile(j):
        return pl.ds(pl.multiple_of(j * 128, 128), 128)

    def fold(value):
        return jnp.sum(value.reshape(16, 8, 128), axis=0)

    barrier = pltpu.get_barrier_semaphore()
    for off in range(1, BAND):
        pl.semaphore_signal(
            barrier, 1, device_id={"band": lax.rem(band + off, BAND)}, device_id_type=MESH
        )
    for off in range(1, DOM):
        pl.semaphore_signal(
            barrier, 1, device_id={"dom": lax.rem(dom + off, DOM)}, device_id_type=MESH
        )
    mine = half_dom == band
    for off in range(DOM):
        source = lax.rem(dom + off, DOM)

        @pl.when(jnp.logical_not(jnp.logical_and(mine, source == dom)))
        def _():
            pl.semaphore_signal(
                barrier, 1, device_id={"band": half_dom, "dom": source}, device_id_type=MESH
            )

    sid_v[...] = lax.shift_right_logical(ordered_v[...], 14)

    occ_of = pairs_v[0:1, :]
    vir_of = pairs_v[1:2, :]
    orbital = iota((64, PAIRS), 0)
    occ_hot = jnp.where(orbital == occ_of, 1.0, 0.0)
    vir_hot = jnp.where(orbital == vir_of + 32, 1.0, 0.0)
    pick_occ[...] = occ_hot.T.astype(BF16)
    pick_vir[...] = vir_hot.T.astype(BF16)
    own = (iota((PAIRS, 128), 1) & 63) + band * OWN == iota((PAIRS, 128), 0)
    own = jnp.where(own, 1.0, 0.0).astype(BF16)
    pick3[:, 0:128] = contract(occ_hot.astype(BF16), own, ((1,), (0,))).astype(BF16)
    pick3[:, 128:256] = contract(vir_hot.astype(BF16), own, ((1,), (0,))).astype(BF16)
    weight_row = iota((64, 128), 0)
    weight_row = jnp.logical_and(weight_row >= 48, weight_row < 51)
    pick3[:, 256:384] = jnp.where(weight_row, 1.0, 0.0).astype(BF16)
    ga[0:128, :] = jnp.zeros((128, 128), F32)
    ga[0:NPC, 0:NPC] = elem_v[...]
    elem = ga[0:128, :]
    elem_high = elem.astype(BF16)
    elem_low = (elem - elem_high.astype(F32)).astype(BF16)
    elem2[...] = jnp.concatenate(
        [
            jnp.concatenate([elem_high, elem_high], axis=1),
            jnp.concatenate([elem_low, elem_low], axis=1),
        ],
        axis=0,
    )
    quad = quad_v[...]
    quad_high = quad.astype(BF16).astype(F32)
    quad_rest = quad - quad_high
    quad_mid = quad_rest.astype(BF16).astype(F32)
    orbf[48 * TILES : 49 * TILES, :] = quad_high
    orbf[49 * TILES : 50 * TILES, :] = quad_mid
    orbf[50 * TILES : 51 * TILES, :] = quad_rest - quad_mid
    orbf[51 * TILES : 64 * TILES, :] = jnp.zeros((13 * TILES, 128), F32)
    ga[120:128, :] = jnp.zeros((8, 128), F32)
    ga[248:256, :] = jnp.zeros((8, 128), F32)
    ga[376:384, :] = jnp.zeros((8, 128), F32)
    ga[504:512, :] = jnp.zeros((8, 128), F32)

    @pl.when(mine)
    def _():
        pl.semaphore_wait(barrier, BAND - 1 + DOM - 1 + DOM - 1)

    @pl.when(jnp.logical_not(mine))
    def _():
        pl.semaphore_wait(barrier, BAND - 1 + DOM - 1 + DOM)

    orb_copies = []
    for off in range(1, BAND):
        copy = pltpu.make_async_remote_copy(
            src_ref=orb_v,
            dst_ref=orb_all.at[band],
            send_sem=orb_ss.at[off],
            recv_sem=orb_rs.at[band],
            device_id={"band": lax.rem(band + off, BAND)},
            device_id_type=MESH,
        )
        copy.start()
        orb_copies.append(copy)
    orb_all[band] = orb_v[...]
    for off in range(1, BAND):
        source = lax.rem(band + off, BAND)
        pltpu.make_async_remote_copy(
            src_ref=orb_v,
            dst_ref=orb_all.at[source],
            send_sem=orb_ss.at[off],
            recv_sem=orb_rs.at[source],
            device_id={"band": source},
            device_id_type=MESH,
        ).wait_recv()
    for b in range(BAND):
        for o in range(4):
            orbf[(4 * b + o) * TILES : (4 * b + o + 1) * TILES, :] = orb_all[b, o].astype(F32)
        for o in range(2):
            at = 32 + 2 * b + o
            orbf[at * TILES : (at + 1) * TILES, :] = orb_all[b, 4 + o].astype(F32)

    def form(group, _):
        for u in range(6):
            j = 6 * group + u
            orbs = orbf[pl.ds(j, 64, stride=TILES), :].astype(BF16)
            rows = contract(orbs, pick3[...], ((0,), (0,)))
            rhs[tile(j), :] = rows[:, 0:128] * rows[:, 128:256] * rows[:, 256:384]
        return 0

    lax.fori_loop(0, TILES // 6, form, 0)

    def renumber(j, _):
        base = pl.multiple_of(j * 128, 128)
        for u in range(128):
            r0[pl.ds(base + u, 1), :] = rhs[pl.ds(old_s[j, u], 1), :]
        return 0

    has_below = dom > 0
    has_above = dom < DOM - 1

    def face_copy(rnd, side, target):
        return pltpu.make_async_remote_copy(
            src_ref=face_send.at[rnd, 1 - side],
            dst_ref=face_recv.at[rnd, side],
            send_sem=face_ss.at[rnd, side],
            recv_sem=face_rs.at[rnd, side],
            device_id={"dom": target},
            device_id_type=MESH,
        )

    def send_faces(rnd):
        @pl.when(has_above)
        def _():
            face_copy(rnd, 0, dom + 1).start()

        @pl.when(has_below)
        def _():
            face_copy(rnd, 1, dom - 1).start()

    def add_faces(rnd, field):
        @pl.when(has_below)
        def _():
            face_copy(rnd, 0, dom - 1).wait_recv()

            def body(j, _):
                got = face_recv[rnd, 0, tile(j), :].astype(F32)
                field[tile(j), :] += got + swap(got)
                return 0

            lax.fori_loop(0, 6, body, 0)

        @pl.when(has_above)
        def _():
            face_copy(rnd, 1, dom + 1).wait_recv()

            def body(j, _):
                got = face_recv[rnd, 1, tile(j), :].astype(F32)
                field[tile(j + 6), :] += got + swap(got)
                return 0

            lax.fori_loop(0, 6, body, 0)

        @pl.when(has_above)
        def _():
            face_copy(rnd, 0, dom + 1).wait_send()

        @pl.when(has_below)
        def _():
            face_copy(rnd, 1, dom - 1).wait_send()

    def pack_faces(rnd, field):
        def body(j, _):
            for side in range(2):
                value = field[tile(j + 6 * side), :]
                face_send[rnd, side, tile(j), :] = halves(value).astype(BF16)
            return 0

        lax.fori_loop(0, 6, body, 0)

    lax.fori_loop(0, 12, renumber, 0)
    pack_faces(0, r0)
    send_faces(0)
    lax.fori_loop(12, TILES, renumber, 0)
    add_faces(0, r0)

    lower_share = jnp.where(has_below, 0.5, 1.0).astype(F32)
    upper_share = jnp.where(has_above, 0.5, 1.0).astype(F32)
    zero_acc = jnp.zeros((8, 128), F32)

    ranges = ((0, 6, lower_share), (6, 12, upper_share), (12, TILES, 1.0))
    rr_part = zero_acc
    for start, stop, share in ranges:

        def start_split(j, acc):
            value = r0[tile(j), :]
            split[tile(j), :] = halves(value)
            return acc + fold(value * value)

        rr_part = rr_part + share * lax.fori_loop(start, stop, start_split, zero_acc)
    rd_part = zero_acc

    index_slots = (index_a, index_b)

    def index_copy(source, chunk, slot):
        rows8 = pl.ds(pl.multiple_of(chunk * 8, 8), 8)
        return pltpu.make_async_copy(
            source.at[rows8, :], index_slots[slot], index_sem.at[slot]
        )

    def stream(source, per_step, fetch, hold, work, init):
        per_chunk = 8 // per_step
        chunks = CELLS // 8
        for slot in range(2):
            index_copy(source, slot, slot).start()
        index_copy(source, 0, 0).wait()
        fetch(index_a, 0)

        def stream_step(i, carry):
            for m in range(2 * per_chunk):
                held = hold()
                slot, row = divmod((m + 1) % (2 * per_chunk), per_chunk)
                if row == 0:
                    index_copy(source, 0, slot).wait()
                fetch(index_slots[slot], row * per_step)
                if row == per_chunk - 1:
                    index_copy(source, lax.rem(2 * i + 2 + slot, chunks), slot).start()
                carry = work(2 * per_chunk * i + m, held, carry)
            return carry

        carry = lax.fori_loop(0, chunks // 2, stream_step, init)
        index_copy(source, 0, 1).wait()
        return carry

    def gather_four(index, row):
        for h in range(4):
            for u in range(NPC):
                ga[pl.ds(128 * h + u, 1), :] = split[pl.ds(index[row + h, u], 1), :]

    def held_four():
        high, low = [], []
        for h in range(2):
            first = ga[256 * h : 256 * h + 128, :]
            second = ga[256 * h + 128 : 256 * h + 256, :]
            high.append(jnp.where(low_half, first, swap(second)).astype(BF16))
            low.append(jnp.where(low_half, swap(first), second).astype(BF16))
        return high, low

    def cell_four(i, held, acc, keep_rows):
        high, low = held
        stacked = jnp.concatenate(
            [jnp.concatenate(high, axis=1), jnp.concatenate(low, axis=1)], axis=0
        )
        product = contract(elem2[...], stacked, ((1,), (0,)))
        product = product[0:128, :] + product[128:256, :]
        for h in range(2):
            cell = 4 * i + 2 * h
            rows = product[:, 128 * h : 128 * h + 128]
            rows = rows * jnp.where(low_half, coef_s[cell], coef_s[cell + 1])
            acc = acc + fold((high[h].astype(F32) + low[h].astype(F32)) * rows)
            if keep_rows:
                turned = swap(rows)
                y_buf[tile(cell), :] = halves(jnp.where(low_half, rows, turned))
                y_buf[tile(cell + 1), :] = halves(jnp.where(low_half, turned, rows))
        return acc

    def cells(keep_rows):
        def cell_work(i, held, acc):
            return cell_four(i, held, acc, keep_rows)

        return stream(node_v, 4, gather_four, held_four, cell_work, zero_acc)

    def one_row(value):
        return jnp.sum(value, axis=0, keepdims=True)

    def send_dots(rnd, rows):
        packed = jnp.concatenate(rows + [jnp.zeros((8 - len(rows), 128), F32)], axis=0)
        dot_send[rnd] = packed
        dot_recv[rnd, dom] = packed
        for off in range(1, DOM):
            pltpu.make_async_remote_copy(
                src_ref=dot_send.at[rnd],
                dst_ref=dot_recv.at[rnd, dom],
                send_sem=dot_ss.at[rnd, off],
                recv_sem=dot_rs.at[rnd, dom],
                device_id={"dom": lax.rem(dom + off, DOM)},
                device_id_type=MESH,
            ).start()

    def sum_dots(rnd):
        for off in range(1, DOM):
            source = lax.rem(dom + off, DOM)
            copy = pltpu.make_async_remote_copy(
                src_ref=dot_send.at[rnd],
                dst_ref=dot_recv.at[rnd, source],
                send_sem=dot_ss.at[rnd, off],
                recv_sem=dot_rs.at[rnd, source],
                device_id={"dom": source},
                device_id_type=MESH,
            )
            copy.wait_recv()
            copy.wait_send()
        total = jnp.sum(dot_recv[rnd], axis=0)
        return [total[k : k + 1, :] for k in range(3)]

    def gather_entries(index, row):
        for h in range(2):
            for u in range(128):
                gx[pl.ds(128 * h + u, 1), :] = y_buf[pl.ds(index[row + h, u], 1), :]

    node_rows = iota((64 * WINDOW, 256), 0)

    def sum_tile(t, held):
        ids = [sid_v[pl.ds(2 * t + h, 1), :] for h in range(2)]
        ids = jnp.concatenate(ids, axis=1) - walk_s[0, t] * 64
        hot = jnp.where(ids == node_rows, 1.0, 0.0).astype(BF16)
        term = contract(hot, held, ((1,), (0,)))
        moved = walk_s[1, t]
        now = [window[moved + k] + term[64 * k : 64 * k + 64] for k in range(WINDOW)]
        for k in range(WINDOW):
            window[k] = now[k]
            sums[t, k] = now[k]

    def sum_entries():
        window[...] = jnp.zeros((2 * WINDOW - 1, 64, 128), F32)

        def hold():
            return gx[...].astype(BF16)

        def entry_work(t, held, carry):
            sum_tile(t, held)
            return carry

        stream(perm_v, 2, gather_entries, hold, entry_work, 0)

    def take(j):
        parts = [sums[walk_s[2, 2 * j + h], walk_s[3, 2 * j + h]] for h in range(2)]
        value = jnp.concatenate(parts, axis=0)
        return value + swap(value)

    def weigh(group, _):
        for u in range(4):
            j = 4 * group + u
            orbs = orbf[pl.ds(j, 64, stride=TILES), :].astype(BF16)
            occ = contract(pick_occ[...], orbs, ((1,), (0,)))
            vir = contract(pick_vir[...], orbs, ((1,), (0,)))
            w_buf[:, tile(j)] = (occ * vir * quad_v[pl.ds(j, 1), :]).astype(BF16)
        return 0

    old_rr = old_den = beta = None
    fields = (r0, r1, r2)
    steps = []
    for it in range(2):
        now, later = fields[it], fields[it + 1]
        quad_part = one_row(cells(True))
        send_dots(it + 1, [one_row(rr_part), one_row(rd_part), quad_part + swap(quad_part)])
        sum_entries()

        def set_faces(j, _):
            value = take(j)
            zf[tile(j), :] = value
            return 0

        lax.fori_loop(0, 12, set_faces, 0)
        pack_faces(it + 1, zf)
        send_faces(it + 1)
        lax.fori_loop(6 * it, 6 * it + 6, weigh, 0)
        rr, rd, quad_form = sum_dots(it + 1)
        if it == 0:
            den = quad_form
        else:
            beta = rr / old_rr
            den = quad_form + 2.0 * beta * rd + beta * beta * old_den
        alpha = rr / den
        steps.append((alpha, beta))

        def advance(j, value, accs, it=it, now=now, later=later, alpha=alpha, beta=beta):
            image = value
            if it == 0:
                im0[tile(j), :] = image
            else:
                image = image + beta * im0[tile(j), :]
            new = now[tile(j), :] - alpha * image
            later[tile(j), :] = new
            split[tile(j), :] = halves(new)
            return accs[0] + fold(new * new), accs[1] + fold(new * image)

        none = (zero_acc, zero_acc)
        rr_part, rd_part = lax.fori_loop(12, TILES, lambda j, a: advance(j, take(j), a), none)
        add_faces(it + 1, zf)
        for start, stop, share in ranges[:2]:
            more = lax.fori_loop(start, stop, lambda j, a: advance(j, zf[tile(j), :], a), none)
            rr_part = rr_part + share * more[0]
            rd_part = rd_part + share * more[1]
        old_rr, old_den = rr, den

    quad_part = one_row(cells(False))
    send_dots(3, [one_row(rr_part), one_row(rd_part), quad_part + swap(quad_part)])
    rr, rd, quad_form = sum_dots(3)
    last_beta = rr / old_rr
    den = quad_form + 2.0 * last_beta * rd + last_beta * last_beta * old_den
    scale2 = rr / den
    scale1 = steps[1][0] + scale2 * last_beta
    scale0 = steps[0][0] + scale1 * steps[1][1]

    def combine(j, _):
        at = tile(j)
        split[at, :] = scale0 * r0[at, :] + scale1 * r1[at, :] + scale2 * r2[at, :]
        return 0

    lax.fori_loop(0, TILES, combine, 0)

    def fetch(j):
        for u in range(128):
            ga[pl.ds(u, 1), :] = split[pl.ds(new_s[j, u], 1), :]

    def deliver(j, value):
        pot16[tile(j), :] = value.astype(BF16)
        pot_out[:, tile(j)] = value.T[0:OWN, :]

    def restore(j, _):
        value = ga[0:128, :]
        fetch(j + 1)
        deliver(j, value)
        return 0

    fetch(0)
    lax.fori_loop(0, TILES - 1, restore, 0)
    deliver(TILES - 1, ga[0:128, :])

    c_acc[...] = jnp.zeros((PAIRS, 128), F32)

    def couple(k, _):
        at = pl.ds(pl.multiple_of(k * 512, 512), 512)
        c_acc[...] += contract(w_buf[:, at], pot16[at, :], ((1,), (0,)))
        return 0

    lax.fori_loop(0, NODES // 512, couple, 0)

    def c_copy(piece, slot, device):
        return pltpu.make_async_remote_copy(
            src_ref=c_send.at[piece],
            dst_ref=c_recv.at[slot],
            send_sem=c_ss.at[piece],
            recv_sem=c_rs.at[slot],
            device_id=device,
            device_id_type=MESH,
        )

    for b in range(BAND):
        block = c_acc[OWN * b : OWN * b + OWN, :]
        turned = jnp.concatenate([block, block], axis=0).T
        for h in range(2):
            piece = 2 * b + h
            c_send[piece] = turned[32 * h : 32 * h + 32, :]
            to_self = jnp.logical_and(band == b, dom == 2 * band + h)

            @pl.when(jnp.logical_not(to_self))
            def _(b=b, h=h, piece=piece):
                c_copy(piece, dom, {"band": b, "dom": 2 * band + h}).start()

            @pl.when(to_self)
            def _(piece=piece):
                c_recv[dom] = c_send[piece]

    for off in range(DOM):
        source = lax.rem(dom + off, DOM)
        from_self = jnp.logical_and(mine, source == dom)

        @pl.when(jnp.logical_not(from_self))
        def _(source=source):
            c_copy(0, source, {"band": half_dom, "dom": source}).wait_recv()

    total = jnp.sum(c_recv[...], axis=0) * (1.0 / (NODES * DOM))
    coup_out[...] = jnp.concatenate([total] * 4, axis=0).T[0:OWN, 0:32]

    for copy in orb_copies:
        copy.wait_send()
    for b in range(BAND):
        for h in range(2):
            piece = 2 * b + h
            to_self = jnp.logical_and(band == b, dom == 2 * band + h)

            @pl.when(jnp.logical_not(to_self))
            def _(b=b, h=h, piece=piece):
                c_copy(piece, dom, {"band": b, "dom": 2 * band + h}).wait_send()


def on_device(
    occ_orb, vir_orb, pair_list, quad_weight, cell_coef, connect, face_map, element_matrix
):
    node, ordered, perm, walk, new, old = build_index(connect, face_map)
    orbs = jnp.concatenate([occ_orb, vir_orb], axis=0).reshape(6, TILES, 128)
    quad = quad_weight.reshape(TILES, 128)
    vmem = pl.BlockSpec(memory_space=pltpu.VMEM)
    smem = pl.BlockSpec(memory_space=pltpu.SMEM)
    dma = pltpu.SemaphoreType.DMA
    field = pltpu.VMEM((NODES, 128), F32)
    return pl.pallas_call(
        main_kernel,
        out_shape=(
            jax.ShapeDtypeStruct((OWN, NODES), F32),
            jax.ShapeDtypeStruct((OWN, 32), F32),
        ),
        in_specs=[smem] * 4 + [vmem] * 7,
        out_specs=(vmem, vmem),
        scratch_shapes=[
            pltpu.VMEM((BAND, 6, TILES, 128), BF16),
            pltpu.VMEM((64 * TILES, 128), F32),
            pltpu.VMEM((64, 384), BF16),
            pltpu.VMEM((PAIRS, 64), BF16),
            pltpu.VMEM((PAIRS, 64), BF16),
            pltpu.VMEM((256, 256), BF16),
            field, field, field, field, field, field,
            pltpu.VMEM((CELLS * 128, 128), F32),
            pltpu.VMEM((256, 128), F32),
            pltpu.VMEM((2 * WINDOW - 1, 64, 128), F32),
            pltpu.VMEM((ENTRY_TILES, WINDOW, 64, 128), F32),
            pltpu.VMEM((PAIRS, NODES), BF16),
            pltpu.VMEM((512, 128), F32),
            pltpu.VMEM((2 * FACE, 128), F32),
            pltpu.VMEM((NODES, 128), BF16),
            pltpu.VMEM((PAIRS, 128), F32),
            pltpu.VMEM((CELLS, 128), I32),
            pltpu.SMEM((8, 128), I32),
            pltpu.SMEM((8, 128), I32),
            pltpu.VMEM((3, 2, FACE, 128), BF16),
            pltpu.VMEM((3, 2, FACE, 128), BF16),
            pltpu.VMEM((4, 8, 128), F32),
            pltpu.VMEM((4, DOM, 8, 128), F32),
            pltpu.VMEM((DOM, 32, 128), F32),
            pltpu.VMEM((DOM, 32, 128), F32),
            dma((BAND,)),
            dma((BAND,)),
            dma((3, 2)),
            dma((3, 2)),
            dma((4, DOM)),
            dma((4, DOM)),
            dma((DOM,)),
            dma((DOM,)),
            dma((2,)),
        ],
        compiler_params=pltpu.CompilerParams(
            collective_id=0, has_side_effects=True, vmem_limit_bytes=60 * 1024 * 1024
        ),
        name="solve",
    )(walk, new, old, cell_coef, node, perm, ordered, orbs, quad, pair_list, element_matrix)


def solution(mesh):
    return jax.shard_map(
        on_device,
        mesh=mesh,
        in_specs=(
            P("band", "dom"),
            P("band", "dom"),
            P(),
            P("dom"),
            P("dom"),
            P(None, "dom"),
            P(None, "dom"),
            P(),
        ),
        out_specs=(P("band", "dom"), P("band", "dom")),
        check_vma=False,
    )
```

```python
import jax
import jax.numpy as jnp
from jax import lax
from jax.experimental import pallas as pl
from jax.experimental.pallas import tpu as pltpu
from jax.sharding import PartitionSpec as P

NODES = 6144
TILES = 48
CELLS = 96
NPC = 125
FACE = 768
BAND = 8
DOM = 16
PAIRS = 512
OWN = 64
ENTRY_TILES = 48
WINDOW = 5
F32 = jnp.float32
BF16 = jnp.bfloat16
I32 = jnp.int32
MESH = pl.DeviceIdType.MESH


def iota(shape, dim):
    return lax.broadcasted_iota(I32, shape, dim)


def contract(first, second, dims):
    return lax.dot_general(first, second, (dims, ((), ())), preferred_element_type=F32)


def index_kernel(
    conn_ref, face_ref, occ_ref, vir_ref,
    key_ref, node_ref, new_ref, old_ref, orb_ref,
    turn, orb_rows, orb_own, orb_all, orb_ss, orb_rs,
):
    band = lax.axis_index("band")
    barrier = pltpu.get_barrier_semaphore()
    for off in range(1, BAND):
        pl.semaphore_signal(
            barrier, 1, device_id={"band": lax.rem(band + off, BAND)}, device_id_type=MESH
        )
    occ = occ_ref[...].astype(F32)
    vir = vir_ref[...].astype(F32)
    for j in range(TILES):
        at = slice(128 * j, 128 * j + 128)
        orb_rows[pl.ds(j, 4, stride=TILES), :] = occ[:, at]
        orb_rows[pl.ds(4 * TILES + j, 2, stride=TILES), :] = vir[:, at]
    orb_own[...] = orb_rows[...].astype(BF16)
    pl.semaphore_wait(barrier, BAND - 1)

    def orb_copy(off, slot, device):
        return pltpu.make_async_remote_copy(
            src_ref=orb_own,
            dst_ref=orb_all.at[slot],
            send_sem=orb_ss.at[off],
            recv_sem=orb_rs.at[slot],
            device_id={"band": device},
            device_id_type=MESH,
        )

    for off in range(1, BAND):
        orb_copy(off, band, lax.rem(band + off, BAND)).start()
    orb_all[band] = orb_own[...]

    rows48 = iota((TILES, 128), 0)
    rows128 = iota((128, 128), 0)
    lane_row = iota((1, 128), 1)

    def table(numbers, base, hit, low):
        high_hot = jnp.where(lax.shift_right_logical(numbers, 7) == rows48, 1.0, 0.0).astype(BF16)
        same = (numbers & 127) == rows128
        low_hot = jnp.where(same, 1.0, 0.0).astype(BF16)
        low_value = jnp.where(same, lane_row, 0).astype(F32).astype(BF16)
        hits = contract(high_hot, low_hot, ((1,), (1,)))
        values = contract(high_hot, low_value, ((1,), (1,)))
        return hit + hits, low + values + base * hits

    turn[...] = jnp.zeros((CELLS, 128), I32)
    turn[:, 0:NPC] = conn_ref[...]
    shared = jnp.zeros((TILES, 128), F32)
    face_id = jnp.zeros((TILES, 128), F32)
    faces = [face_ref[k : k + 1, 128 * j : 128 * j + 128] for k in range(2) for j in range(6)]
    for j in range(2 * FACE // 128):
        shared, face_id = table(faces[j], 128.0 * j, shared, face_id)
    inner = 1.0 - shared
    inner16 = inner.astype(BF16)
    before = jnp.where(iota((128, 128), 0) < iota((128, 128), 1), 1.0, 0.0).astype(BF16)
    above = jnp.where(iota((TILES, TILES), 1) < iota((TILES, TILES), 0), 1.0, 0.0).astype(BF16)
    in_row = contract(inner16, before, ((1,), (0,)))
    rows_above = jnp.sum(contract(above, inner16, ((1,), (0,))), axis=1, keepdims=True)
    number = jnp.where(shared > 0.5, face_id, in_row + rows_above + 2.0 * FACE)
    new_ref[...] = number.astype(I32)

    def invert(group, carry):
        hit, low = carry
        for u in range(8):
            base = (1024 * group + 128 * u).astype(F32)
            hit, low = table(new_ref[pl.ds(8 * group + u, 1), :], base, hit, low)
        return hit, low

    zero = jnp.zeros((TILES, 128), F32)
    _, old = lax.fori_loop(0, TILES // 8, invert, (zero, zero))
    old_ref[...] = old.astype(I32)

    number_int = number.astype(I32)
    high_part = lax.shift_right_logical(number_int, 7).astype(F32)
    low_part = (number_int & 127).astype(F32)
    parts = jnp.concatenate([high_part, low_part], axis=1).T.astype(BF16)

    def look_up(group, _):
        found = []
        for u in range(8):
            nodes = turn[pl.ds(group * 8 + u, 1), :]
            hot = jnp.where(lax.shift_right_logical(nodes, 7) == rows48, 1.0, 0.0).astype(BF16)
            both = contract(parts, hot, ((1,), (0,)))
            value = 128.0 * both[:128] + both[128:]
            same = (nodes & 127) == rows128
            found.append(jnp.sum(jnp.where(same, value, 0.0), axis=0, keepdims=True))
        ids = jnp.concatenate(found, axis=0).astype(I32)
        lanes = iota((8, 128), 1)
        code = (iota((8, 128), 0) + group * 8) * 128 + lanes
        real = lanes < NPC
        at = pl.ds(pl.multiple_of(group * 8, 8), 8)
        key_ref[at, :] = jnp.where(real, ids, NODES) * 16384 + code
        node_ref[at, :] = jnp.where(real, ids, 0)
        return 0

    lax.fori_loop(0, CELLS // 8, look_up, 0)
    for off in range(1, BAND):
        source = lax.rem(band + off, BAND)
        orb_copy(off, source, source).wait_recv()
    orb_ref[...] = orb_all[...]
    for off in range(1, BAND):
        orb_copy(off, band, lax.rem(band + off, BAND)).wait_send()


def build_index(connect, face_map, occ_orb, vir_orb):
    vmem = pl.BlockSpec(memory_space=pltpu.VMEM)
    shape = jax.ShapeDtypeStruct
    dma = pltpu.SemaphoreType.DMA
    key, node, new, old, orbs = pl.pallas_call(
        index_kernel,
        out_shape=[
            shape((CELLS, 128), I32),
            shape((CELLS, 128), I32),
            shape((TILES, 128), I32),
            shape((TILES, 128), I32),
            shape((BAND, 6 * TILES, 128), BF16),
        ],
        in_specs=[vmem] * 4,
        out_specs=[vmem] * 5,
        scratch_shapes=[
            pltpu.VMEM((CELLS, 128), I32),
            pltpu.VMEM((6 * TILES, 128), F32),
            pltpu.VMEM((6 * TILES, 128), BF16),
            pltpu.VMEM((BAND, 6 * TILES, 128), BF16),
            dma((BAND,)),
            dma((BAND,)),
        ],
        compiler_params=pltpu.CompilerParams(
            collective_id=1, has_side_effects=True, vmem_limit_bytes=32 * 1024 * 1024
        ),
        name="index",
    )(connect.T, face_map, occ_orb, vir_orb)
    ordered = lax.sort(key.reshape(CELLS * 128), is_stable=False).reshape(CELLS, 128)
    block = lax.shift_right_logical(ordered[0:94:2, 0], 20)
    place = jnp.arange(128, dtype=I32)
    begins = block[None, :] <= place[:, None]
    last_tile = jnp.sum(begins.astype(I32), axis=1) - 1
    last_block = jnp.max(jnp.where(begins, block[None, :], 0), axis=1)
    within = jnp.clip(place - last_block, 0, WINDOW - 1)
    move = jnp.clip(block - jnp.concatenate([block[:1], block[:-1]]), 0, WINDOW - 1)
    walk = jnp.stack(
        [jnp.pad(block, (0, 81)), jnp.pad(move, (0, 81)), jnp.clip(last_tile, 0, 46), within]
    )
    return node, ordered, ordered & 16383, walk, new, old, orbs


def main_kernel(
    walk_s, new_s, old_s, coef_s,
    node_v, perm_v, ordered_v, orb_v, quad_v, pairs_v, elem_v,
    pot_out, coup_out,
    orbf, pick3, pick_occ, pick_vir, elem2,
    rhs, r0, r1, r2, im0, split, y_buf, gx, window, sums, w_buf, ga, zf, pot16, c_acc, sid_v, index_a, index_b,
    face_send, face_recv, dot_send, dot_recv, c_send, c_recv,
    face_ss, face_rs, dot_ss, dot_rs, c_ss, c_rs, index_sem,
):
    dom = lax.axis_index("dom")
    band = lax.axis_index("band")
    half_dom = lax.div(dom, 2)
    low_half = iota((128, 128), 1) < 64

    def swap(value):
        return pltpu.roll(value, 64, 1)

    def halves(value):
        high = value.astype(BF16).astype(F32)
        return jnp.where(low_half, high, value - high)

    def tile(j):
        return pl.ds(pl.multiple_of(j * 128, 128), 128)

    def fold(value):
        return jnp.sum(value.reshape(16, 8, 128), axis=0)

    barrier = pltpu.get_barrier_semaphore()
    for off in range(1, DOM):
        pl.semaphore_signal(
            barrier, 1, device_id={"dom": lax.rem(dom + off, DOM)}, device_id_type=MESH
        )
    mine = half_dom == band
    for off in range(DOM):
        source = lax.rem(dom + off, DOM)

        @pl.when(jnp.logical_not(jnp.logical_and(mine, source == dom)))
        def _():
            pl.semaphore_signal(
                barrier, 1, device_id={"band": half_dom, "dom": source}, device_id_type=MESH
            )

    sid_v[...] = lax.shift_right_logical(ordered_v[...], 14)

    occ_of = pairs_v[0:1, :]
    vir_of = pairs_v[1:2, :]
    orbital = iota((64, PAIRS), 0)
    occ_hot = jnp.where(orbital == occ_of, 1.0, 0.0)
    vir_hot = jnp.where(orbital == vir_of + 32, 1.0, 0.0)
    pick_occ[...] = occ_hot.T.astype(BF16)
    pick_vir[...] = vir_hot.T.astype(BF16)
    own = (iota((PAIRS, 128), 1) & 63) + band * OWN == iota((PAIRS, 128), 0)
    own = jnp.where(own, 1.0, 0.0).astype(BF16)
    pick3[:, 0:128] = contract(occ_hot.astype(BF16), own, ((1,), (0,))).astype(BF16)
    pick3[:, 128:256] = contract(vir_hot.astype(BF16), own, ((1,), (0,))).astype(BF16)
    weight_row = iota((64, 128), 0)
    weight_row = jnp.logical_and(weight_row >= 48, weight_row < 51)
    pick3[:, 256:384] = jnp.where(weight_row, 1.0, 0.0).astype(BF16)
    ga[0:128, :] = jnp.zeros((128, 128), F32)
    ga[0:NPC, 0:NPC] = elem_v[...]
    elem = ga[0:128, :]
    elem_high = elem.astype(BF16)
    elem_low = (elem - elem_high.astype(F32)).astype(BF16)
    elem2[...] = jnp.concatenate(
        [
            jnp.concatenate([elem_high, elem_high], axis=1),
            jnp.concatenate([elem_low, elem_low], axis=1),
        ],
        axis=0,
    )
    quad = quad_v[...]
    quad_high = quad.astype(BF16).astype(F32)
    quad_rest = quad - quad_high
    quad_mid = quad_rest.astype(BF16).astype(F32)
    orbf[48 * TILES : 49 * TILES, :] = quad_high
    orbf[49 * TILES : 50 * TILES, :] = quad_mid
    orbf[50 * TILES : 51 * TILES, :] = quad_rest - quad_mid
    orbf[51 * TILES : 64 * TILES, :] = jnp.zeros((13 * TILES, 128), F32)
    ga[120:128, :] = jnp.zeros((8, 128), F32)
    ga[248:256, :] = jnp.zeros((8, 128), F32)
    ga[376:384, :] = jnp.zeros((8, 128), F32)
    ga[504:512, :] = jnp.zeros((8, 128), F32)

    for b in range(BAND):
        for o in range(4):
            orbf[(4 * b + o) * TILES : (4 * b + o + 1) * TILES, :] = orb_v[b, o * TILES : (o + 1) * TILES].astype(F32)
        for o in range(2):
            at = 32 + 2 * b + o
            orbf[at * TILES : (at + 1) * TILES, :] = orb_v[b, (4 + o) * TILES : (5 + o) * TILES].astype(F32)

    def form(group, _):
        for u in range(6):
            j = 6 * group + u
            orbs = orbf[pl.ds(j, 64, stride=TILES), :].astype(BF16)
            rows = contract(orbs, pick3[...], ((0,), (0,)))
            rhs[tile(j), :] = rows[:, 0:128] * rows[:, 128:256] * rows[:, 256:384]
        return 0

    lax.fori_loop(0, TILES // 6, form, 0)

    def renumber(j, _):
        base = pl.multiple_of(j * 128, 128)
        for u in range(128):
            r0[pl.ds(base + u, 1), :] = rhs[pl.ds(old_s[j, u], 1), :]
        return 0

    has_below = dom > 0
    has_above = dom < DOM - 1

    def face_copy(rnd, side, target):
        return pltpu.make_async_remote_copy(
            src_ref=face_send.at[rnd, 1 - side],
            dst_ref=face_recv.at[rnd, side],
            send_sem=face_ss.at[rnd, side],
            recv_sem=face_rs.at[rnd, side],
            device_id={"dom": target},
            device_id_type=MESH,
        )

    def send_faces(rnd):
        @pl.when(has_above)
        def _():
            face_copy(rnd, 0, dom + 1).start()

        @pl.when(has_below)
        def _():
            face_copy(rnd, 1, dom - 1).start()

    def add_faces(rnd, field):
        @pl.when(has_below)
        def _():
            face_copy(rnd, 0, dom - 1).wait_recv()

            def body(j, _):
                got = face_recv[rnd, 0, tile(j), :].astype(F32)
                field[tile(j), :] += got + swap(got)
                return 0

            lax.fori_loop(0, 6, body, 0)

        @pl.when(has_above)
        def _():
            face_copy(rnd, 1, dom + 1).wait_recv()

            def body(j, _):
                got = face_recv[rnd, 1, tile(j), :].astype(F32)
                field[tile(j + 6), :] += got + swap(got)
                return 0

            lax.fori_loop(0, 6, body, 0)

        @pl.when(has_above)
        def _():
            face_copy(rnd, 0, dom + 1).wait_send()

        @pl.when(has_below)
        def _():
            face_copy(rnd, 1, dom - 1).wait_send()

    def pack_faces(rnd, field):
        def body(j, _):
            for side in range(2):
                value = field[tile(j + 6 * side), :]
                face_send[rnd, side, tile(j), :] = halves(value).astype(BF16)
            return 0

        lax.fori_loop(0, 6, body, 0)

    lax.fori_loop(0, 12, renumber, 0)
    pack_faces(0, r0)
    @pl.when(mine)
    def _():
        pl.semaphore_wait(barrier, DOM - 1 + DOM - 1)

    @pl.when(jnp.logical_not(mine))
    def _():
        pl.semaphore_wait(barrier, DOM - 1 + DOM)

    send_faces(0)
    lax.fori_loop(12, TILES, renumber, 0)
    add_faces(0, r0)

    lower_share = jnp.where(has_below, 0.5, 1.0).astype(F32)
    upper_share = jnp.where(has_above, 0.5, 1.0).astype(F32)
    zero_acc = jnp.zeros((8, 128), F32)

    ranges = ((0, 6, lower_share), (6, 12, upper_share), (12, TILES, 1.0))
    rr_part = zero_acc
    for start, stop, share in ranges:

        def start_split(j, acc):
            value = r0[tile(j), :]
            split[tile(j), :] = halves(value)
            return acc + fold(value * value)

        rr_part = rr_part + share * lax.fori_loop(start, stop, start_split, zero_acc)
    rd_part = zero_acc

    index_slots = (index_a, index_b)

    def index_copy(source, chunk, slot):
        rows8 = pl.ds(pl.multiple_of(chunk * 8, 8), 8)
        return pltpu.make_async_copy(
            source.at[rows8, :], index_slots[slot], index_sem.at[slot]
        )

    def stream(source, per_step, fetch, hold, work, init):
        per_chunk = 8 // per_step
        chunks = CELLS // 8
        for slot in range(2):
            index_copy(source, slot, slot).start()
        index_copy(source, 0, 0).wait()
        fetch(index_a, 0)

        def stream_step(i, carry):
            for m in range(2 * per_chunk):
                held = hold()
                slot, row = divmod((m + 1) % (2 * per_chunk), per_chunk)
                if row == 0:
                    index_copy(source, 0, slot).wait()
                fetch(index_slots[slot], row * per_step)
                if row == per_chunk - 1:
                    index_copy(source, lax.rem(2 * i + 2 + slot, chunks), slot).start()
                carry = work(2 * per_chunk * i + m, held, carry)
            return carry

        carry = lax.fori_loop(0, chunks // 2, stream_step, init)
        index_copy(source, 0, 1).wait()
        return carry

    def gather_four(index, row):
        for h in range(4):
            for u in range(NPC):
                ga[pl.ds(128 * h + u, 1), :] = split[pl.ds(index[row + h, u], 1), :]

    def held_four():
        high, low = [], []
        for h in range(2):
            first = ga[256 * h : 256 * h + 128, :]
            second = ga[256 * h + 128 : 256 * h + 256, :]
            high.append(jnp.where(low_half, first, swap(second)).astype(BF16))
            low.append(jnp.where(low_half, swap(first), second).astype(BF16))
        return high, low

    def cell_four(i, held, acc, keep_rows):
        high, low = held
        stacked = jnp.concatenate(
            [jnp.concatenate(high, axis=1), jnp.concatenate(low, axis=1)], axis=0
        )
        product = contract(elem2[...], stacked, ((1,), (0,)))
        product = product[0:128, :] + product[128:256, :]
        for h in range(2):
            cell = 4 * i + 2 * h
            rows = product[:, 128 * h : 128 * h + 128]
            rows = rows * jnp.where(low_half, coef_s[cell], coef_s[cell + 1])
            acc = acc + fold((high[h].astype(F32) + low[h].astype(F32)) * rows)
            if keep_rows:
                turned = swap(rows)
                y_buf[tile(cell), :] = halves(jnp.where(low_half, rows, turned))
                y_buf[tile(cell + 1), :] = halves(jnp.where(low_half, turned, rows))
        return acc

    def cells(keep_rows):
        def cell_work(i, held, acc):
            return cell_four(i, held, acc, keep_rows)

        return stream(node_v, 4, gather_four, held_four, cell_work, zero_acc)

    def one_row(value):
        return jnp.sum(value, axis=0, keepdims=True)

    def send_dots(rnd, rows):
        packed = jnp.concatenate(rows + [jnp.zeros((8 - len(rows), 128), F32)], axis=0)
        dot_send[rnd] = packed
        dot_recv[rnd, dom] = packed
        for off in range(1, DOM):
            pltpu.make_async_remote_copy(
                src_ref=dot_send.at[rnd],
                dst_ref=dot_recv.at[rnd, dom],
                send_sem=dot_ss.at[rnd, off],
                recv_sem=dot_rs.at[rnd, dom],
                device_id={"dom": lax.rem(dom + off, DOM)},
                device_id_type=MESH,
            ).start()

    def sum_dots(rnd):
        for off in range(1, DOM):
            source = lax.rem(dom + off, DOM)
            copy = pltpu.make_async_remote_copy(
                src_ref=dot_send.at[rnd],
                dst_ref=dot_recv.at[rnd, source],
                send_sem=dot_ss.at[rnd, off],
                recv_sem=dot_rs.at[rnd, source],
                device_id={"dom": source},
                device_id_type=MESH,
            )
            copy.wait_recv()
            copy.wait_send()
        total = jnp.sum(dot_recv[rnd], axis=0)
        return [total[k : k + 1, :] for k in range(3)]

    def gather_entries(index, row):
        for h in range(2):
            for u in range(128):
                gx[pl.ds(128 * h + u, 1), :] = y_buf[pl.ds(index[row + h, u], 1), :]

    node_rows = iota((64 * WINDOW, 256), 0)

    def sum_tile(t, held):
        ids = [sid_v[pl.ds(2 * t + h, 1), :] for h in range(2)]
        ids = jnp.concatenate(ids, axis=1) - walk_s[0, t] * 64
        hot = jnp.where(ids == node_rows, 1.0, 0.0).astype(BF16)
        term = contract(hot, held, ((1,), (0,)))
        moved = walk_s[1, t]
        now = [window[moved + k] + term[64 * k : 64 * k + 64] for k in range(WINDOW)]
        for k in range(WINDOW):
            window[k] = now[k]
            sums[t, k] = now[k]

    def sum_entries():
        window[...] = jnp.zeros((2 * WINDOW - 1, 64, 128), F32)

        def hold():
            return gx[...].astype(BF16)

        def entry_work(t, held, carry):
            sum_tile(t, held)
            return carry

        stream(perm_v, 2, gather_entries, hold, entry_work, 0)

    def take(j):
        parts = [sums[walk_s[2, 2 * j + h], walk_s[3, 2 * j + h]] for h in range(2)]
        value = jnp.concatenate(parts, axis=0)
        return value + swap(value)

    def weigh(group, _):
        for u in range(4):
            j = 4 * group + u
            orbs = orbf[pl.ds(j, 64, stride=TILES), :].astype(BF16)
            occ = contract(pick_occ[...], orbs, ((1,), (0,)))
            vir = contract(pick_vir[...], orbs, ((1,), (0,)))
            w_buf[:, tile(j)] = (occ * vir * quad_v[pl.ds(j, 1), :]).astype(BF16)
        return 0

    old_rr = old_den = beta = None
    fields = (r0, r1, r2)
    steps = []
    for it in range(2):
        now, later = fields[it], fields[it + 1]
        quad_part = one_row(cells(True))
        send_dots(it + 1, [one_row(rr_part), one_row(rd_part), quad_part + swap(quad_part)])
        sum_entries()

        def set_faces(j, _):
            value = take(j)
            zf[tile(j), :] = value
            return 0

        lax.fori_loop(0, 12, set_faces, 0)
        pack_faces(it + 1, zf)
        send_faces(it + 1)
        lax.fori_loop(4 * it, 4 * it + 4, weigh, 0)
        rr, rd, quad_form = sum_dots(it + 1)
        if it == 0:
            den = quad_form
        else:
            beta = rr / old_rr
            den = quad_form + 2.0 * beta * rd + beta * beta * old_den
        alpha = rr / den
        steps.append((alpha, beta))

        def advance(j, value, accs, it=it, now=now, later=later, alpha=alpha, beta=beta):
            image = value
            if it == 0:
                im0[tile(j), :] = image
            else:
                image = image + beta * im0[tile(j), :]
            new = now[tile(j), :] - alpha * image
            later[tile(j), :] = new
            split[tile(j), :] = halves(new)
            return accs[0] + fold(new * new), accs[1] + fold(new * image)

        none = (zero_acc, zero_acc)

        def inner(group, accs):
            for u in range(3):
                j = 3 * group + u
                accs = advance(j, take(j), accs)
            return accs

        rr_part, rd_part = lax.fori_loop(4, TILES // 3, inner, none)
        add_faces(it + 1, zf)
        for start, stop, share in ranges[:2]:

            def outer(group, accs):
                for u in range(3):
                    j = 3 * group + u
                    accs = advance(j, zf[tile(j), :], accs)
                return accs

            more = lax.fori_loop(start // 3, stop // 3, outer, none)
            rr_part = rr_part + share * more[0]
            rd_part = rd_part + share * more[1]
        old_rr, old_den = rr, den

    quad_part = one_row(cells(False))
    send_dots(3, [one_row(rr_part), one_row(rd_part), quad_part + swap(quad_part)])
    lax.fori_loop(8, 12, weigh, 0)
    rr, rd, quad_form = sum_dots(3)
    last_beta = rr / old_rr
    den = quad_form + 2.0 * last_beta * rd + last_beta * last_beta * old_den
    scale2 = rr / den
    scale1 = steps[1][0] + scale2 * last_beta
    scale0 = steps[0][0] + scale1 * steps[1][1]

    def combine(j, _):
        at = tile(j)
        split[at, :] = scale0 * r0[at, :] + scale1 * r1[at, :] + scale2 * r2[at, :]
        return 0

    lax.fori_loop(0, TILES, combine, 0)

    def fetch(j):
        for u in range(128):
            ga[pl.ds(u, 1), :] = split[pl.ds(new_s[j, u], 1), :]

    def deliver(j, value):
        pot16[tile(j), :] = value.astype(BF16)
        pot_out[:, tile(j)] = value.T[0:OWN, :]

    def restore(j, _):
        value = ga[0:128, :]
        fetch(j + 1)
        deliver(j, value)
        return 0

    fetch(0)
    lax.fori_loop(0, TILES - 1, restore, 0)
    deliver(TILES - 1, ga[0:128, :])

    c_acc[...] = jnp.zeros((PAIRS, 128), F32)

    def couple(k, _):
        at = pl.ds(pl.multiple_of(k * 512, 512), 512)
        c_acc[...] += contract(w_buf[:, at], pot16[at, :], ((1,), (0,)))
        return 0

    lax.fori_loop(0, NODES // 512, couple, 0)

    def c_copy(piece, slot, device):
        return pltpu.make_async_remote_copy(
            src_ref=c_send.at[piece],
            dst_ref=c_recv.at[slot],
            send_sem=c_ss.at[piece],
            recv_sem=c_rs.at[slot],
            device_id=device,
            device_id_type=MESH,
        )

    for b in range(BAND):
        block = c_acc[OWN * b : OWN * b + OWN, :]
        turned = jnp.concatenate([block, block], axis=0).T
        for h in range(2):
            piece = 2 * b + h
            upper = turned[32 * h : 32 * h + 16, :]
            lower = turned[32 * h + 16 : 32 * h + 32, :]
            c_send[piece] = jnp.where(low_half[0:16, :], upper, lower)
            to_self = jnp.logical_and(band == b, dom == 2 * band + h)

            @pl.when(jnp.logical_not(to_self))
            def _(b=b, h=h, piece=piece):
                c_copy(piece, dom, {"band": b, "dom": 2 * band + h}).start()

            @pl.when(to_self)
            def _(piece=piece):
                c_recv[dom] = c_send[piece]

    for off in range(DOM):
        source = lax.rem(dom + off, DOM)
        from_self = jnp.logical_and(mine, source == dom)

        @pl.when(jnp.logical_not(from_self))
        def _(source=source):
            c_copy(0, source, {"band": half_dom, "dom": source}).wait_recv()

    total = jnp.sum(c_recv[...], axis=0) * (1.0 / (NODES * DOM))
    coup_out[...] = jnp.concatenate([total, swap(total)], axis=0)[:, 0:OWN]

    for b in range(BAND):
        for h in range(2):
            piece = 2 * b + h
            to_self = jnp.logical_and(band == b, dom == 2 * band + h)

            @pl.when(jnp.logical_not(to_self))
            def _(b=b, h=h, piece=piece):
                c_copy(piece, dom, {"band": b, "dom": 2 * band + h}).wait_send()


def on_device(
    occ_orb, vir_orb, pair_list, quad_weight, cell_coef, connect, face_map, element_matrix
):
    index = build_index(connect, face_map, occ_orb, vir_orb)
    node, ordered, perm, walk, new, old, orbs = index
    quad = quad_weight.reshape(TILES, 128)
    vmem = pl.BlockSpec(memory_space=pltpu.VMEM)
    smem = pl.BlockSpec(memory_space=pltpu.SMEM)
    dma = pltpu.SemaphoreType.DMA
    field = pltpu.VMEM((NODES, 128), F32)
    potential, coupling = pl.pallas_call(
        main_kernel,
        out_shape=(
            jax.ShapeDtypeStruct((OWN, NODES), F32),
            jax.ShapeDtypeStruct((32, OWN), F32),
        ),
        in_specs=[smem] * 4 + [vmem] * 7,
        out_specs=(vmem, vmem),
        scratch_shapes=[
            pltpu.VMEM((64 * TILES, 128), F32),
            pltpu.VMEM((64, 384), BF16),
            pltpu.VMEM((PAIRS, 64), BF16),
            pltpu.VMEM((PAIRS, 64), BF16),
            pltpu.VMEM((256, 256), BF16),
            field, field, field, field, field, field,
            pltpu.VMEM((CELLS * 128, 128), F32),
            pltpu.VMEM((256, 128), F32),
            pltpu.VMEM((2 * WINDOW - 1, 64, 128), F32),
            pltpu.VMEM((ENTRY_TILES, WINDOW, 64, 128), F32),
            pltpu.VMEM((PAIRS, NODES), BF16),
            pltpu.VMEM((512, 128), F32),
            pltpu.VMEM((2 * FACE, 128), F32),
            pltpu.VMEM((NODES, 128), BF16),
            pltpu.VMEM((PAIRS, 128), F32),
            pltpu.VMEM((CELLS, 128), I32),
            pltpu.SMEM((8, 128), I32),
            pltpu.SMEM((8, 128), I32),
            pltpu.VMEM((3, 2, FACE, 128), BF16),
            pltpu.VMEM((3, 2, FACE, 128), BF16),
            pltpu.VMEM((4, 8, 128), F32),
            pltpu.VMEM((4, DOM, 8, 128), F32),
            pltpu.VMEM((DOM, 16, 128), F32),
            pltpu.VMEM((DOM, 16, 128), F32),
            dma((3, 2)),
            dma((3, 2)),
            dma((4, DOM)),
            dma((4, DOM)),
            dma((DOM,)),
            dma((DOM,)),
            dma((2,)),
        ],
        compiler_params=pltpu.CompilerParams(
            collective_id=0, has_side_effects=True, vmem_limit_bytes=60 * 1024 * 1024
        ),
        name="solve",
    )(walk, new, old, cell_coef, node, perm, ordered, orbs, quad, pair_list, element_matrix)
    return potential, coupling.T


def solution(mesh):
    return jax.shard_map(
        on_device,
        mesh=mesh,
        in_specs=(
            P("band", "dom"),
            P("band", "dom"),
            P(),
            P("dom"),
            P("dom"),
            P(None, "dom"),
            P(None, "dom"),
            P(),
        ),
        out_specs=(P("band", "dom"), P("band", "dom")),
        check_vma=False,
    )
```

```python
import jax
import jax.numpy as jnp
from jax import lax
from jax.experimental import pallas as pl
from jax.experimental.pallas import tpu as pltpu
from jax.sharding import PartitionSpec as P

NODES = 6144
TILES = 48
CELLS = 96
NPC = 125
FACE = 768
BAND = 8
DOM = 16
PAIRS = 512
OWN = 64
ENTRY_TILES = 48
WINDOW = 5
F32 = jnp.float32
BF16 = jnp.bfloat16
I32 = jnp.int32
MESH = pl.DeviceIdType.MESH


def iota(shape, dim):
    return lax.broadcasted_iota(I32, shape, dim)


def contract(first, second, dims):
    return lax.dot_general(first, second, (dims, ((), ())), preferred_element_type=F32)


def index_kernel(
    conn_ref, face_ref, occ_ref, vir_ref,
    key_ref, node_ref, new_ref, old_ref, orb_ref,
    turn, orb_rows, orb_own, orb_all, orb_ss, orb_rs,
):
    band = lax.axis_index("band")
    barrier = pltpu.get_barrier_semaphore()
    for off in range(1, BAND):
        pl.semaphore_signal(
            barrier, 1, device_id={"band": lax.rem(band + off, BAND)}, device_id_type=MESH
        )
    occ = occ_ref[...].astype(F32)
    vir = vir_ref[...].astype(F32)
    for j in range(TILES):
        at = slice(128 * j, 128 * j + 128)
        orb_rows[pl.ds(j, 4, stride=TILES), :] = occ[:, at]
        orb_rows[pl.ds(4 * TILES + j, 2, stride=TILES), :] = vir[:, at]
    orb_own[...] = orb_rows[...].astype(BF16)
    pl.semaphore_wait(barrier, BAND - 1)

    def orb_copy(off, slot, device):
        return pltpu.make_async_remote_copy(
            src_ref=orb_own,
            dst_ref=orb_all.at[slot],
            send_sem=orb_ss.at[off],
            recv_sem=orb_rs.at[slot],
            device_id={"band": device},
            device_id_type=MESH,
        )

    for off in range(1, BAND):
        orb_copy(off, band, lax.rem(band + off, BAND)).start()
    orb_all[band] = orb_own[...]

    rows48 = iota((TILES, 128), 0)
    rows128 = iota((128, 128), 0)
    lane_row = iota((1, 128), 1)

    def table(numbers, base, hit, low):
        high_hot = jnp.where(lax.shift_right_logical(numbers, 7) == rows48, 1.0, 0.0).astype(BF16)
        same = (numbers & 127) == rows128
        low_hot = jnp.where(same, 1.0, 0.0).astype(BF16)
        low_value = jnp.where(same, lane_row, 0).astype(F32).astype(BF16)
        hits = contract(high_hot, low_hot, ((1,), (1,)))
        values = contract(high_hot, low_value, ((1,), (1,)))
        return hit + hits, low + values + base * hits

    turn[...] = jnp.zeros((CELLS, 128), I32)
    turn[:, 0:NPC] = conn_ref[...]
    shared = jnp.zeros((TILES, 128), F32)
    face_id = jnp.zeros((TILES, 128), F32)
    faces = [face_ref[k : k + 1, 128 * j : 128 * j + 128] for k in range(2) for j in range(6)]
    for j in range(2 * FACE // 128):
        shared, face_id = table(faces[j], 128.0 * j, shared, face_id)
    inner = 1.0 - shared
    inner16 = inner.astype(BF16)
    before = jnp.where(iota((128, 128), 0) < iota((128, 128), 1), 1.0, 0.0).astype(BF16)
    above = jnp.where(iota((TILES, TILES), 1) < iota((TILES, TILES), 0), 1.0, 0.0).astype(BF16)
    in_row = contract(inner16, before, ((1,), (0,)))
    rows_above = jnp.sum(contract(above, inner16, ((1,), (0,))), axis=1, keepdims=True)
    number = jnp.where(shared > 0.5, face_id, in_row + rows_above + 2.0 * FACE)
    new_ref[...] = number.astype(I32)

    def invert(group, carry):
        hit, low = carry
        for u in range(8):
            base = (1024 * group + 128 * u).astype(F32)
            hit, low = table(new_ref[pl.ds(8 * group + u, 1), :], base, hit, low)
        return hit, low

    zero = jnp.zeros((TILES, 128), F32)
    _, old = lax.fori_loop(0, TILES // 8, invert, (zero, zero))
    old_ref[...] = old.astype(I32)

    number_int = number.astype(I32)
    high_part = lax.shift_right_logical(number_int, 7).astype(F32)
    low_part = (number_int & 127).astype(F32)
    parts = jnp.concatenate([high_part, low_part], axis=1).T.astype(BF16)

    def look_up(group, _):
        found = []
        for u in range(8):
            nodes = turn[pl.ds(group * 8 + u, 1), :]
            hot = jnp.where(lax.shift_right_logical(nodes, 7) == rows48, 1.0, 0.0).astype(BF16)
            both = contract(parts, hot, ((1,), (0,)))
            value = 128.0 * both[:128] + both[128:]
            same = (nodes & 127) == rows128
            found.append(jnp.sum(jnp.where(same, value, 0.0), axis=0, keepdims=True))
        ids = jnp.concatenate(found, axis=0).astype(I32)
        lanes = iota((8, 128), 1)
        code = (iota((8, 128), 0) + group * 8) * 128 + lanes
        real = lanes < NPC
        at = pl.ds(pl.multiple_of(group * 8, 8), 8)
        key_ref[at, :] = jnp.where(real, ids, NODES) * 16384 + code
        node_ref[at, :] = jnp.where(real, ids, 0)
        return 0

    lax.fori_loop(0, CELLS // 8, look_up, 0)
    for off in range(1, BAND):
        source = lax.rem(band + off, BAND)
        orb_copy(off, source, source).wait_recv()
    orb_ref[...] = orb_all[...]
    for off in range(1, BAND):
        orb_copy(off, band, lax.rem(band + off, BAND)).wait_send()


def build_index(connect, face_map, occ_orb, vir_orb):
    vmem = pl.BlockSpec(memory_space=pltpu.VMEM)
    shape = jax.ShapeDtypeStruct
    dma = pltpu.SemaphoreType.DMA
    key, node, new, old, orbs = pl.pallas_call(
        index_kernel,
        out_shape=[
            shape((CELLS, 128), I32),
            shape((CELLS, 128), I32),
            shape((TILES, 128), I32),
            shape((TILES, 128), I32),
            shape((BAND, 6 * TILES, 128), BF16),
        ],
        in_specs=[vmem] * 4,
        out_specs=[vmem] * 5,
        scratch_shapes=[
            pltpu.VMEM((CELLS, 128), I32),
            pltpu.VMEM((6 * TILES, 128), F32),
            pltpu.VMEM((6 * TILES, 128), BF16),
            pltpu.VMEM((BAND, 6 * TILES, 128), BF16),
            dma((BAND,)),
            dma((BAND,)),
        ],
        compiler_params=pltpu.CompilerParams(
            collective_id=1, has_side_effects=True, vmem_limit_bytes=60 * 1024 * 1024
        ),
        name="index",
    )(connect.T, face_map, occ_orb, vir_orb)
    ordered = lax.sort(key.reshape(CELLS * 128), is_stable=False).reshape(CELLS, 128)
    block = lax.shift_right_logical(ordered[0:94:2, 0], 20)
    place = jnp.arange(128, dtype=I32)
    begins = block[None, :] <= place[:, None]
    last_tile = jnp.sum(begins.astype(I32), axis=1) - 1
    last_block = jnp.max(jnp.where(begins, block[None, :], 0), axis=1)
    within = jnp.clip(place - last_block, 0, WINDOW - 1)
    move = jnp.clip(block - jnp.concatenate([block[:1], block[:-1]]), 0, WINDOW - 1)
    walk = jnp.stack(
        [jnp.pad(block, (0, 81)), jnp.pad(move, (0, 81)), jnp.clip(last_tile, 0, 46), within]
    )
    return node, ordered, ordered & 16383, walk, new, old, orbs


def main_kernel(
    walk_s, new_s, old_s, coef_s,
    node_v, perm_v, ordered_v, orb_v, quad_v, pairs_v, elem_v,
    pot_out, coup_out,
    orbf, pick3, pick_occ, pick_vir, elem2,
    rhs, r0, r1, r2, im0, split, y_buf, gx, window, sums, terms, products, whole, w_buf, ga, zf, c_acc, sid_v, index_a, index_b,
    face_send, face_recv, dot_send, dot_recv, c_send, c_recv,
    face_ss, face_rs, dot_ss, dot_rs, c_ss, c_rs, index_sem,
):
    dom = lax.axis_index("dom")
    band = lax.axis_index("band")
    half_dom = lax.div(dom, 2)
    low_half = iota((128, 128), 1) < 64

    def swap(value):
        return pltpu.roll(value, 64, 1)

    def halves(value):
        high = value.astype(BF16).astype(F32)
        return jnp.where(low_half, high, value - high)

    def tile(j):
        return pl.ds(pl.multiple_of(j * 128, 128), 128)

    def fold(value):
        return jnp.sum(value.reshape(16, 8, 128), axis=0)

    barrier = pltpu.get_barrier_semaphore()
    for off in range(1, DOM):
        pl.semaphore_signal(
            barrier, 1, device_id={"dom": lax.rem(dom + off, DOM)}, device_id_type=MESH
        )
    mine = half_dom == band
    for off in range(DOM):
        source = lax.rem(dom + off, DOM)

        @pl.when(jnp.logical_not(jnp.logical_and(mine, source == dom)))
        def _():
            pl.semaphore_signal(
                barrier, 1, device_id={"band": half_dom, "dom": source}, device_id_type=MESH
            )

    sid_v[...] = lax.shift_right_logical(ordered_v[...], 14)

    occ_of = pairs_v[0:1, :]
    vir_of = pairs_v[1:2, :]
    orbital = iota((64, PAIRS), 0)
    occ_hot = jnp.where(orbital == occ_of, 1.0, 0.0)
    vir_hot = jnp.where(orbital == vir_of + 32, 1.0, 0.0)
    pick_occ[...] = occ_hot.T.astype(BF16)
    pick_vir[...] = vir_hot.T.astype(BF16)
    own = (iota((PAIRS, 128), 1) & 63) + band * OWN == iota((PAIRS, 128), 0)
    own = jnp.where(own, 1.0, 0.0).astype(BF16)
    pick3[:, 0:128] = contract(occ_hot.astype(BF16), own, ((1,), (0,))).astype(BF16)
    pick3[:, 128:256] = contract(vir_hot.astype(BF16), own, ((1,), (0,))).astype(BF16)
    weight_row = iota((64, 128), 0)
    weight_row = jnp.logical_and(weight_row >= 48, weight_row < 51)
    pick3[:, 256:384] = jnp.where(weight_row, 1.0, 0.0).astype(BF16)
    ga[0:128, :] = jnp.zeros((128, 128), F32)
    ga[0:NPC, 0:NPC] = elem_v[...]
    elem = ga[0:128, :]
    elem_high = elem.astype(BF16)
    elem_low = (elem - elem_high.astype(F32)).astype(BF16)
    elem2[...] = jnp.concatenate(
        [
            jnp.concatenate([elem_high, elem_high], axis=1),
            jnp.concatenate([elem_low, elem_low], axis=1),
        ],
        axis=0,
    )
    quad = quad_v[...]
    quad_high = quad.astype(BF16).astype(F32)
    quad_rest = quad - quad_high
    quad_mid = quad_rest.astype(BF16).astype(F32)
    orbf[48 * TILES : 49 * TILES, :] = quad_high
    orbf[49 * TILES : 50 * TILES, :] = quad_mid
    orbf[50 * TILES : 51 * TILES, :] = quad_rest - quad_mid
    orbf[51 * TILES : 64 * TILES, :] = jnp.zeros((13 * TILES, 128), F32)
    ga[120:128, :] = jnp.zeros((8, 128), F32)
    ga[248:256, :] = jnp.zeros((8, 128), F32)
    ga[376:384, :] = jnp.zeros((8, 128), F32)
    ga[504:512, :] = jnp.zeros((8, 128), F32)

    for b in range(BAND):
        for o in range(4):
            orbf[(4 * b + o) * TILES : (4 * b + o + 1) * TILES, :] = orb_v[b, o * TILES : (o + 1) * TILES].astype(F32)
        for o in range(2):
            at = 32 + 2 * b + o
            orbf[at * TILES : (at + 1) * TILES, :] = orb_v[b, (4 + o) * TILES : (5 + o) * TILES].astype(F32)

    def form(group, _):
        for u in range(6):
            j = 6 * group + u
            orbs = orbf[pl.ds(j, 64, stride=TILES), :].astype(BF16)
            rows = contract(orbs, pick3[...], ((0,), (0,)))
            rhs[tile(j), :] = rows[:, 0:128] * rows[:, 128:256] * rows[:, 256:384]
        return 0

    lax.fori_loop(0, TILES // 6, form, 0)

    def weigh(group, _):
        for u in range(4):
            j = 4 * group + u
            orbs = orbf[pl.ds(j, 64, stride=TILES), :].astype(BF16)
            occ = contract(pick_occ[...], orbs, ((1,), (0,)))
            vir = contract(pick_vir[...], orbs, ((1,), (0,)))
            w_buf[:, tile(j)] = (occ * vir * quad_v[pl.ds(j, 1), :]).astype(BF16)
        return 0

    def renumber(j, _):
        base = pl.multiple_of(j * 128, 128)
        for u in range(128):
            r0[pl.ds(base + u, 1), :] = rhs[pl.ds(old_s[j, u], 1), :]
        return 0

    has_below = dom > 0
    has_above = dom < DOM - 1

    def face_copy(rnd, side, target):
        return pltpu.make_async_remote_copy(
            src_ref=face_send.at[rnd, 1 - side],
            dst_ref=face_recv.at[rnd, side],
            send_sem=face_ss.at[rnd, side],
            recv_sem=face_rs.at[rnd, side],
            device_id={"dom": target},
            device_id_type=MESH,
        )

    def send_faces(rnd):
        @pl.when(has_above)
        def _():
            face_copy(rnd, 0, dom + 1).start()

        @pl.when(has_below)
        def _():
            face_copy(rnd, 1, dom - 1).start()

    def add_faces(rnd, field):
        @pl.when(has_below)
        def _():
            face_copy(rnd, 0, dom - 1).wait_recv()

            def body(j, _):
                got = face_recv[rnd, 0, tile(j), :].astype(F32)
                field[tile(j), :] += got + swap(got)
                return 0

            lax.fori_loop(0, 6, body, 0)

        @pl.when(has_above)
        def _():
            face_copy(rnd, 1, dom + 1).wait_recv()

            def body(j, _):
                got = face_recv[rnd, 1, tile(j), :].astype(F32)
                field[tile(j + 6), :] += got + swap(got)
                return 0

            lax.fori_loop(0, 6, body, 0)

        @pl.when(has_above)
        def _():
            face_copy(rnd, 0, dom + 1).wait_send()

        @pl.when(has_below)
        def _():
            face_copy(rnd, 1, dom - 1).wait_send()

    def pack_faces(rnd, field):
        def body(j, _):
            for side in range(2):
                value = field[tile(j + 6 * side), :]
                face_send[rnd, side, tile(j), :] = halves(value).astype(BF16)
            return 0

        lax.fori_loop(0, 6, body, 0)

    lax.fori_loop(0, 12, renumber, 0)
    pack_faces(0, r0)
    @pl.when(mine)
    def _():
        pl.semaphore_wait(barrier, DOM - 1 + DOM - 1)

    @pl.when(jnp.logical_not(mine))
    def _():
        pl.semaphore_wait(barrier, DOM - 1 + DOM)

    send_faces(0)
    lax.fori_loop(12, TILES, renumber, 0)
    lax.fori_loop(0, 3, weigh, 0)
    add_faces(0, r0)

    lower_share = jnp.where(has_below, 0.5, 1.0).astype(F32)
    upper_share = jnp.where(has_above, 0.5, 1.0).astype(F32)
    zero_acc = jnp.zeros((8, 128), F32)

    ranges = ((0, 6, lower_share), (6, 12, upper_share), (12, TILES, 1.0))
    rr_part = zero_acc
    for start, stop, share in ranges:

        def start_split(j, acc):
            value = r0[tile(j), :]
            split[tile(j), :] = halves(value)
            return acc + fold(value * value)

        rr_part = rr_part + share * lax.fori_loop(start, stop, start_split, zero_acc)
    rd_part = zero_acc

    place8 = iota((8, 128), 0)

    def rows_of(source, index, row, start, count=8):
        merged = None
        for u in range(count):
            at = pl.ds(index[row, start + u], 1)
            spread = jnp.broadcast_to(source[at, :], (8, 128))
            merged = spread if u == 0 else jnp.where(place8 == u, spread, merged)
        return merged

    index_slots = (index_a, index_b)

    def index_copy(source, chunk, slot):
        rows8 = pl.ds(pl.multiple_of(chunk * 8, 8), 8)
        return pltpu.make_async_copy(
            source.at[rows8, :], index_slots[slot], index_sem.at[slot]
        )

    def stream(source, per_step, fetch, hold, work, finish, init):
        per_chunk = 8 // per_step
        steps = CELLS // per_step
        chunks = CELLS // 8
        for slot in range(2):
            index_copy(source, slot, slot).start()
        index_copy(source, 0, 0).wait()
        fetch(index_a, 0)

        def stream_step(i, carry):
            for m in range(2 * per_chunk):
                step = 2 * per_chunk * i + m
                slot, row = divmod((m + 1) % (2 * per_chunk), per_chunk)
                if row == 0:
                    index_copy(source, 0, slot).wait()
                carry = finish(lax.rem(step + steps - 1, steps), carry)
                held = hold()
                fetch(index_slots[slot], row * per_step)
                work(step, held)
                if row == per_chunk - 1:
                    index_copy(source, lax.rem(2 * i + 2 + slot, chunks), slot).start()
            return carry

        carry = lax.fori_loop(0, chunks // 2, stream_step, init)
        index_copy(source, 0, 1).wait()
        return finish(steps - 1, carry)

    def gather_four(index, row):
        for h in range(4):
            for u in range(0, 128, 8):
                count = min(8, NPC - u)
                ga[pl.ds(128 * h + u, 8), :] = rows_of(split, index, row + h, u, count)

    def held_four():
        high, low = [], []
        for h in range(2):
            first = ga[256 * h : 256 * h + 128, :]
            second = ga[256 * h + 128 : 256 * h + 256, :]
            high.append(jnp.where(low_half, first, swap(second)).astype(BF16))
            low.append(jnp.where(low_half, swap(first), second).astype(BF16))
        return high, low

    def cell_work(i, held):
        high, low = held
        stacked = jnp.concatenate(
            [jnp.concatenate(high, axis=1), jnp.concatenate(low, axis=1)], axis=0
        )
        product = contract(elem2[...], stacked, ((1,), (0,)))
        products[...] = product[0:128, :] + product[128:256, :]
        for h in range(2):
            whole[:, 128 * h : 128 * h + 128] = high[h].astype(F32) + low[h].astype(F32)

    def cells(keep_rows):
        products[...] = jnp.zeros((128, 256), F32)
        whole[...] = jnp.zeros((128, 256), F32)

        def cell_finish(i, acc):
            for h in range(2):
                cell = 4 * i + 2 * h
                at = slice(128 * h, 128 * h + 128)
                rows = products[:, at] * jnp.where(low_half, coef_s[cell], coef_s[cell + 1])
                acc = acc + fold(whole[:, at] * rows)
                if keep_rows:
                    turned = swap(rows)
                    y_buf[tile(cell), :] = halves(jnp.where(low_half, rows, turned))
                    y_buf[tile(cell + 1), :] = halves(jnp.where(low_half, turned, rows))
            return acc

        return stream(node_v, 4, gather_four, held_four, cell_work, cell_finish, zero_acc)

    def one_row(value):
        return jnp.sum(value, axis=0, keepdims=True)

    def send_dots(rnd, rows):
        packed = jnp.concatenate(rows + [jnp.zeros((8 - len(rows), 128), F32)], axis=0)
        dot_send[rnd] = packed
        dot_recv[rnd, dom] = packed
        for off in range(1, DOM):
            pltpu.make_async_remote_copy(
                src_ref=dot_send.at[rnd],
                dst_ref=dot_recv.at[rnd, dom],
                send_sem=dot_ss.at[rnd, off],
                recv_sem=dot_rs.at[rnd, dom],
                device_id={"dom": lax.rem(dom + off, DOM)},
                device_id_type=MESH,
            ).start()

    def sum_dots(rnd):
        for off in range(1, DOM):
            source = lax.rem(dom + off, DOM)
            copy = pltpu.make_async_remote_copy(
                src_ref=dot_send.at[rnd],
                dst_ref=dot_recv.at[rnd, source],
                send_sem=dot_ss.at[rnd, off],
                recv_sem=dot_rs.at[rnd, source],
                device_id={"dom": source},
                device_id_type=MESH,
            )
            copy.wait_recv()
            copy.wait_send()
        total = jnp.sum(dot_recv[rnd], axis=0)
        return [total[k : k + 1, :] for k in range(3)]

    def gather_entries(index, row):
        for h in range(2):
            for u in range(0, 128, 8):
                gx[pl.ds(128 * h + u, 8), :] = rows_of(y_buf, index, row + h, u)

    node_rows = iota((64 * WINDOW, 256), 0)

    def entry_work(t, held):
        ids = [sid_v[pl.ds(2 * t + h, 1), :] for h in range(2)]
        ids = jnp.concatenate(ids, axis=1) - walk_s[0, t] * 64
        hot = jnp.where(ids == node_rows, 1.0, 0.0).astype(BF16)
        terms[...] = contract(hot, held, ((1,), (0,)))

    def entry_finish(t, carry):
        moved = walk_s[1, t]
        now = [window[moved + k] + terms[64 * k : 64 * k + 64, :] for k in range(WINDOW)]
        for k in range(WINDOW):
            window[k] = now[k]
            sums[t, k] = now[k]
        return carry

    def sum_entries():
        window[...] = jnp.zeros((2 * WINDOW - 1, 64, 128), F32)
        terms[...] = jnp.zeros((64 * WINDOW, 128), F32)

        def hold():
            return gx[...].astype(BF16)

        stream(perm_v, 2, gather_entries, hold, entry_work, entry_finish, 0)

    def take(j):
        parts = [sums[walk_s[2, 2 * j + h], walk_s[3, 2 * j + h]] for h in range(2)]
        value = jnp.concatenate(parts, axis=0)
        return value + swap(value)

    old_rr = old_den = beta = None
    fields = (r0, r1, r2)
    steps = []
    for it in range(2):
        now, later = fields[it], fields[it + 1]
        quad_part = one_row(cells(True))
        send_dots(it + 1, [one_row(rr_part), one_row(rd_part), quad_part + swap(quad_part)])
        sum_entries()

        def set_faces(j, _):
            value = take(j)
            zf[tile(j), :] = value
            return 0

        lax.fori_loop(0, 12, set_faces, 0)
        pack_faces(it + 1, zf)
        send_faces(it + 1)
        lax.fori_loop(3 * it + 3, 3 * it + 6, weigh, 0)
        rr, rd, quad_form = sum_dots(it + 1)
        if it == 0:
            den = quad_form
        else:
            beta = rr / old_rr
            den = quad_form + 2.0 * beta * rd + beta * beta * old_den
        alpha = rr / den
        steps.append((alpha, beta))

        def advance(j, value, accs, it=it, now=now, later=later, alpha=alpha, beta=beta):
            image = value
            if it == 0:
                im0[tile(j), :] = image
            else:
                image = image + beta * im0[tile(j), :]
            new = now[tile(j), :] - alpha * image
            later[tile(j), :] = new
            split[tile(j), :] = halves(new)
            return accs[0] + fold(new * new), accs[1] + fold(new * image)

        none = (zero_acc, zero_acc)

        def inner(group, accs):
            for u in range(3):
                j = 3 * group + u
                accs = advance(j, take(j), accs)
            return accs

        rr_part, rd_part = lax.fori_loop(4, TILES // 3, inner, none)
        add_faces(it + 1, zf)
        for start, stop, share in ranges[:2]:

            def outer(group, accs):
                for u in range(3):
                    j = 3 * group + u
                    accs = advance(j, zf[tile(j), :], accs)
                return accs

            more = lax.fori_loop(start // 3, stop // 3, outer, none)
            rr_part = rr_part + share * more[0]
            rd_part = rd_part + share * more[1]
        old_rr, old_den = rr, den

    quad_part = one_row(cells(False))
    send_dots(3, [one_row(rr_part), one_row(rd_part), quad_part + swap(quad_part)])
    lax.fori_loop(9, 12, weigh, 0)
    rr, rd, quad_form = sum_dots(3)
    last_beta = rr / old_rr
    den = quad_form + 2.0 * last_beta * rd + last_beta * last_beta * old_den
    scale2 = rr / den
    scale1 = steps[1][0] + scale2 * last_beta
    scale0 = steps[0][0] + scale1 * steps[1][1]

    def combine(j, _):
        at = tile(j)
        split[at, :] = scale0 * r0[at, :] + scale1 * r1[at, :] + scale2 * r2[at, :]
        return 0

    lax.fori_loop(0, TILES, combine, 0)

    def restore(j, _):
        base = pl.multiple_of(j * 128, 128)
        for u in range(128):
            rhs[pl.ds(base + u, 1), :] = split[pl.ds(new_s[j, u], 1), :]
        return 0

    lax.fori_loop(0, TILES, restore, 0)

    c_acc[...] = jnp.zeros((PAIRS, 128), F32)

    def couple(k, _):
        at = pl.ds(pl.multiple_of(k * 512, 512), 512)
        c_acc[...] += contract(w_buf[:, at], rhs[at, :].astype(BF16), ((1,), (0,)))
        return 0

    lax.fori_loop(0, NODES // 512, couple, 0)

    def c_copy(piece, slot, device):
        return pltpu.make_async_remote_copy(
            src_ref=c_send.at[piece],
            dst_ref=c_recv.at[slot],
            send_sem=c_ss.at[piece],
            recv_sem=c_rs.at[slot],
            device_id=device,
            device_id_type=MESH,
        )

    for b in range(BAND):
        block = c_acc[OWN * b : OWN * b + OWN, :]
        turned = jnp.concatenate([block, block], axis=0).T
        for h in range(2):
            piece = 2 * b + h
            upper = turned[32 * h : 32 * h + 16, :]
            lower = turned[32 * h + 16 : 32 * h + 32, :]
            c_send[piece] = jnp.where(low_half[0:16, :], upper, lower)
            to_self = jnp.logical_and(band == b, dom == 2 * band + h)

            @pl.when(jnp.logical_not(to_self))
            def _(b=b, h=h, piece=piece):
                c_copy(piece, dom, {"band": b, "dom": 2 * band + h}).start()

            @pl.when(to_self)
            def _(piece=piece):
                c_recv[dom] = c_send[piece]

    def deliver(group, _):
        for u in range(4):
            j = 4 * group + u
            pot_out[:, tile(j)] = rhs[tile(j), :].T[0:OWN, :]
        return 0

    lax.fori_loop(0, TILES // 4, deliver, 0)

    for off in range(DOM):
        source = lax.rem(dom + off, DOM)
        from_self = jnp.logical_and(mine, source == dom)

        @pl.when(jnp.logical_not(from_self))
        def _(source=source):
            c_copy(0, source, {"band": half_dom, "dom": source}).wait_recv()

    total = jnp.sum(c_recv[...], axis=0) * (1.0 / (NODES * DOM))
    coup_out[...] = jnp.concatenate([total, swap(total)], axis=0)[:, 0:OWN]

    for b in range(BAND):
        for h in range(2):
            piece = 2 * b + h
            to_self = jnp.logical_and(band == b, dom == 2 * band + h)

            @pl.when(jnp.logical_not(to_self))
            def _(b=b, h=h, piece=piece):
                c_copy(piece, dom, {"band": b, "dom": 2 * band + h}).wait_send()


def on_device(
    occ_orb, vir_orb, pair_list, quad_weight, cell_coef, connect, face_map, element_matrix
):
    index = build_index(connect, face_map, occ_orb, vir_orb)
    node, ordered, perm, walk, new, old, orbs = index
    quad = quad_weight.reshape(TILES, 128)
    vmem = pl.BlockSpec(memory_space=pltpu.VMEM)
    smem = pl.BlockSpec(memory_space=pltpu.SMEM)
    dma = pltpu.SemaphoreType.DMA
    field = pltpu.VMEM((NODES, 128), F32)
    potential, coupling = pl.pallas_call(
        main_kernel,
        out_shape=(
            jax.ShapeDtypeStruct((OWN, NODES), F32),
            jax.ShapeDtypeStruct((32, OWN), F32),
        ),
        in_specs=[smem] * 4 + [vmem] * 7,
        out_specs=(vmem, vmem),
        scratch_shapes=[
            pltpu.VMEM((64 * TILES, 128), F32),
            pltpu.VMEM((64, 384), BF16),
            pltpu.VMEM((PAIRS, 64), BF16),
            pltpu.VMEM((PAIRS, 64), BF16),
            pltpu.VMEM((256, 256), BF16),
            field, field, field, field, field, field,
            pltpu.VMEM((CELLS * 128, 128), F32),
            pltpu.VMEM((256, 128), F32),
            pltpu.VMEM((2 * WINDOW - 1, 64, 128), F32),
            pltpu.VMEM((ENTRY_TILES, WINDOW, 64, 128), F32),
            pltpu.VMEM((64 * WINDOW, 128), F32),
            pltpu.VMEM((128, 256), F32),
            pltpu.VMEM((128, 256), F32),
            pltpu.VMEM((PAIRS, NODES), BF16),
            pltpu.VMEM((512, 128), F32),
            pltpu.VMEM((2 * FACE, 128), F32),
            pltpu.VMEM((PAIRS, 128), F32),
            pltpu.VMEM((CELLS, 128), I32),
            pltpu.SMEM((8, 128), I32),
            pltpu.SMEM((8, 128), I32),
            pltpu.VMEM((3, 2, FACE, 128), BF16),
            pltpu.VMEM((3, 2, FACE, 128), BF16),
            pltpu.VMEM((4, 8, 128), F32),
            pltpu.VMEM((4, DOM, 8, 128), F32),
            pltpu.VMEM((DOM, 16, 128), F32),
            pltpu.VMEM((DOM, 16, 128), F32),
            dma((3, 2)),
            dma((3, 2)),
            dma((4, DOM)),
            dma((4, DOM)),
            dma((DOM,)),
            dma((DOM,)),
            dma((2,)),
        ],
        compiler_params=pltpu.CompilerParams(
            collective_id=0, has_side_effects=True, vmem_limit_bytes=60 * 1024 * 1024
        ),
        name="solve",
    )(walk, new, old, cell_coef, node, perm, ordered, orbs, quad, pair_list, element_matrix)
    return potential, coupling.T


def solution(mesh):
    return jax.shard_map(
        on_device,
        mesh=mesh,
        in_specs=(
            P("band", "dom"),
            P("band", "dom"),
            P(),
            P("dom"),
            P("dom"),
            P(None, "dom"),
            P(None, "dom"),
            P(),
        ),
        out_specs=(P("band", "dom"), P("band", "dom")),
        check_vma=False,
    )
```

```python
import jax
import jax.numpy as jnp
from jax import lax
from jax.experimental import pallas as pl
from jax.experimental.pallas import tpu as pltpu
from jax.sharding import PartitionSpec as P

NODES = 6144
TILES = 48
CELLS = 96
NPC = 125
FACE = 768
BAND = 8
DOM = 16
PAIRS = 512
OWN = 64
ENTRY_TILES = 48
WINDOW = 5
F32 = jnp.float32
BF16 = jnp.bfloat16
I32 = jnp.int32
MESH = pl.DeviceIdType.MESH


def iota(shape, dim):
    return lax.broadcasted_iota(I32, shape, dim)


def contract(first, second, dims):
    return lax.dot_general(first, second, (dims, ((), ())), preferred_element_type=F32)


def index_kernel(
    conn_ref, face_ref, occ_ref, vir_ref,
    key_ref, node_ref, new_ref, old_ref, orb_ref,
    turn, orb_rows, orb_own, orb_all, orb_ss, orb_rs,
):
    band = lax.axis_index("band")
    barrier = pltpu.get_barrier_semaphore()
    for off in range(1, BAND):
        pl.semaphore_signal(
            barrier, 1, device_id={"band": lax.rem(band + off, BAND)}, device_id_type=MESH
        )
    occ = occ_ref[...].astype(F32)
    vir = vir_ref[...].astype(F32)
    for j in range(TILES):
        at = slice(128 * j, 128 * j + 128)
        orb_rows[pl.ds(j, 4, stride=TILES), :] = occ[:, at]
        orb_rows[pl.ds(4 * TILES + j, 2, stride=TILES), :] = vir[:, at]
    orb_own[...] = orb_rows[...].astype(BF16)
    pl.semaphore_wait(barrier, BAND - 1)

    def orb_copy(off, slot, device):
        return pltpu.make_async_remote_copy(
            src_ref=orb_own,
            dst_ref=orb_all.at[slot],
            send_sem=orb_ss.at[off],
            recv_sem=orb_rs.at[slot],
            device_id={"band": device},
            device_id_type=MESH,
        )

    for off in range(1, BAND):
        orb_copy(off, band, lax.rem(band + off, BAND)).start()
    orb_all[band] = orb_own[...]

    rows48 = iota((TILES, 128), 0)
    rows128 = iota((128, 128), 0)
    lane_row = iota((1, 128), 1)

    def table(numbers, base, hit, low):
        high_hot = jnp.where(lax.shift_right_logical(numbers, 7) == rows48, 1.0, 0.0).astype(BF16)
        same = (numbers & 127) == rows128
        low_hot = jnp.where(same, 1.0, 0.0).astype(BF16)
        low_value = jnp.where(same, lane_row, 0).astype(F32).astype(BF16)
        hits = contract(high_hot, low_hot, ((1,), (1,)))
        values = contract(high_hot, low_value, ((1,), (1,)))
        return hit + hits, low + values + base * hits

    turn[...] = jnp.zeros((CELLS, 128), I32)
    turn[:, 0:NPC] = conn_ref[...]
    shared = jnp.zeros((TILES, 128), F32)
    face_id = jnp.zeros((TILES, 128), F32)
    faces = [face_ref[k : k + 1, 128 * j : 128 * j + 128] for k in range(2) for j in range(6)]
    for j in range(2 * FACE // 128):
        shared, face_id = table(faces[j], 128.0 * j, shared, face_id)
    inner = 1.0 - shared
    inner16 = inner.astype(BF16)
    before = jnp.where(iota((128, 128), 0) < iota((128, 128), 1), 1.0, 0.0).astype(BF16)
    above = jnp.where(iota((TILES, TILES), 1) < iota((TILES, TILES), 0), 1.0, 0.0).astype(BF16)
    in_row = contract(inner16, before, ((1,), (0,)))
    rows_above = jnp.sum(contract(above, inner16, ((1,), (0,))), axis=1, keepdims=True)
    number = jnp.where(shared > 0.5, face_id, in_row + rows_above + 2.0 * FACE)
    new_ref[...] = number.astype(I32)

    def invert(group, carry):
        hit, low = carry
        for u in range(8):
            base = (1024 * group + 128 * u).astype(F32)
            hit, low = table(new_ref[pl.ds(8 * group + u, 1), :], base, hit, low)
        return hit, low

    zero = jnp.zeros((TILES, 128), F32)
    _, old = lax.fori_loop(0, TILES // 8, invert, (zero, zero))
    old_ref[...] = old.astype(I32)

    number_int = number.astype(I32)
    high_part = lax.shift_right_logical(number_int, 7).astype(F32)
    low_part = (number_int & 127).astype(F32)
    parts = jnp.concatenate([high_part, low_part], axis=1).T.astype(BF16)

    def look_up(group, _):
        found = []
        for u in range(8):
            nodes = turn[pl.ds(group * 8 + u, 1), :]
            hot = jnp.where(lax.shift_right_logical(nodes, 7) == rows48, 1.0, 0.0).astype(BF16)
            both = contract(parts, hot, ((1,), (0,)))
            value = 128.0 * both[:128] + both[128:]
            same = (nodes & 127) == rows128
            found.append(jnp.sum(jnp.where(same, value, 0.0), axis=0, keepdims=True))
        ids = jnp.concatenate(found, axis=0).astype(I32)
        lanes = iota((8, 128), 1)
        code = (iota((8, 128), 0) + group * 8) * 128 + lanes
        real = lanes < NPC
        at = pl.ds(pl.multiple_of(group * 8, 8), 8)
        key_ref[at, :] = jnp.where(real, ids, NODES) * 16384 + code
        node_ref[at, :] = jnp.where(real, ids, 0)
        return 0

    lax.fori_loop(0, CELLS // 8, look_up, 0)
    for off in range(1, BAND):
        source = lax.rem(band + off, BAND)
        orb_copy(off, source, source).wait_recv()
    orb_ref[...] = orb_all[...]
    for off in range(1, BAND):
        orb_copy(off, band, lax.rem(band + off, BAND)).wait_send()


def build_index(connect, face_map, occ_orb, vir_orb):
    vmem = pl.BlockSpec(memory_space=pltpu.VMEM)
    shape = jax.ShapeDtypeStruct
    dma = pltpu.SemaphoreType.DMA
    key, node, new, old, orbs = pl.pallas_call(
        index_kernel,
        out_shape=[
            shape((CELLS, 128), I32),
            shape((CELLS, 128), I32),
            shape((TILES, 128), I32),
            shape((TILES, 128), I32),
            shape((BAND, 6 * TILES, 128), BF16),
        ],
        in_specs=[vmem] * 4,
        out_specs=[vmem] * 5,
        scratch_shapes=[
            pltpu.VMEM((CELLS, 128), I32),
            pltpu.VMEM((6 * TILES, 128), F32),
            pltpu.VMEM((6 * TILES, 128), BF16),
            pltpu.VMEM((BAND, 6 * TILES, 128), BF16),
            dma((BAND,)),
            dma((BAND,)),
        ],
        compiler_params=pltpu.CompilerParams(
            collective_id=1, has_side_effects=True, vmem_limit_bytes=60 * 1024 * 1024
        ),
        name="index",
    )(connect.T, face_map, occ_orb, vir_orb)
    ordered = lax.sort(key.reshape(CELLS * 128), is_stable=False).reshape(CELLS, 128)
    block = lax.shift_right_logical(ordered[0:94:2, 0], 20)
    place = jnp.arange(128, dtype=I32)
    begins = block[None, :] <= place[:, None]
    last_tile = jnp.sum(begins.astype(I32), axis=1) - 1
    last_block = jnp.max(jnp.where(begins, block[None, :], 0), axis=1)
    within = jnp.clip(place - last_block, 0, WINDOW - 1)
    move = jnp.clip(block[1:] - block[:-1], 0, WINDOW - 1)
    walk = jnp.stack(
        [jnp.pad(block, (0, 81)), jnp.pad(move, (1, 81)), jnp.clip(last_tile, 0, 46), within]
    )
    return node, ordered, ordered & 16383, walk, new, old, orbs


def main_kernel(
    walk_s, coef_s,
    new_v, old_v, node_v, perm_v, ordered_v, orb_v, quad_v, pairs_v, elem_v,
    pot_out, coup_out,
    orbf, pick3, pick_occ, pick_vir, elem2,
    rhs, r0, r1, r2, im0, split, y_buf, gx, window, sums, terms, products, whole, w_buf, ga, zf, c_acc, sid_v, index_a, index_b,
    face_send, face_recv, dot_send, dot_recv, c_send, c_recv,
    face_ss, face_rs, dot_ss, dot_rs, c_ss, c_rs, index_sem,
):
    dom = lax.axis_index("dom")
    band = lax.axis_index("band")
    half_dom = lax.div(dom, 2)
    low_half = iota((128, 128), 1) < 64

    def swap(value):
        return pltpu.roll(value, 64, 1)

    def halves(value):
        high = value.astype(BF16).astype(F32)
        return jnp.where(low_half, high, value - high)

    def tile(j):
        return pl.ds(pl.multiple_of(j * 128, 128), 128)

    def fold(value):
        return jnp.sum(value.reshape(16, 8, 128), axis=0)

    barrier = pltpu.get_barrier_semaphore()
    for off in range(1, DOM):
        pl.semaphore_signal(
            barrier, 1, device_id={"dom": lax.rem(dom + off, DOM)}, device_id_type=MESH
        )
    mine = half_dom == band
    for off in range(DOM):
        source = lax.rem(dom + off, DOM)

        @pl.when(jnp.logical_not(jnp.logical_and(mine, source == dom)))
        def _():
            pl.semaphore_signal(
                barrier, 1, device_id={"band": half_dom, "dom": source}, device_id_type=MESH
            )

    sid_v[...] = lax.shift_right_logical(ordered_v[...], 14)

    occ_of = pairs_v[0:1, :]
    vir_of = pairs_v[1:2, :]
    orbital = iota((64, PAIRS), 0)
    occ_hot = jnp.where(orbital == occ_of, 1.0, 0.0)
    vir_hot = jnp.where(orbital == vir_of + 32, 1.0, 0.0)
    pick_occ[...] = occ_hot.T.astype(BF16)
    pick_vir[...] = vir_hot.T.astype(BF16)
    own = (iota((PAIRS, 128), 1) & 63) + band * OWN == iota((PAIRS, 128), 0)
    own = jnp.where(own, 1.0, 0.0).astype(BF16)
    pick3[:, 0:128] = contract(occ_hot.astype(BF16), own, ((1,), (0,))).astype(BF16)
    pick3[:, 128:256] = contract(vir_hot.astype(BF16), own, ((1,), (0,))).astype(BF16)
    weight_row = iota((64, 128), 0)
    weight_row = jnp.logical_and(weight_row >= 48, weight_row < 51)
    pick3[:, 256:384] = jnp.where(weight_row, 1.0, 0.0).astype(BF16)
    ga[0:128, :] = jnp.zeros((128, 128), F32)
    ga[0:NPC, 0:NPC] = elem_v[...]
    elem = ga[0:128, :]
    elem_high = elem.astype(BF16)
    elem_low = (elem - elem_high.astype(F32)).astype(BF16)
    elem2[...] = jnp.concatenate(
        [
            jnp.concatenate([elem_high, elem_high], axis=1),
            jnp.concatenate([elem_low, elem_low], axis=1),
        ],
        axis=0,
    )
    quad = quad_v[...]
    quad_high = quad.astype(BF16).astype(F32)
    quad_rest = quad - quad_high
    quad_mid = quad_rest.astype(BF16).astype(F32)
    orbf[48 * TILES : 49 * TILES, :] = quad_high
    orbf[49 * TILES : 50 * TILES, :] = quad_mid
    orbf[50 * TILES : 51 * TILES, :] = quad_rest - quad_mid
    orbf[51 * TILES : 64 * TILES, :] = jnp.zeros((13 * TILES, 128), F32)
    ga[120:128, :] = jnp.zeros((8, 128), F32)
    ga[248:256, :] = jnp.zeros((8, 128), F32)
    ga[376:384, :] = jnp.zeros((8, 128), F32)
    ga[504:512, :] = jnp.zeros((8, 128), F32)

    for b in range(BAND):
        for o in range(4):
            orbf[(4 * b + o) * TILES : (4 * b + o + 1) * TILES, :] = orb_v[b, o * TILES : (o + 1) * TILES].astype(F32)
        for o in range(2):
            at = 32 + 2 * b + o
            orbf[at * TILES : (at + 1) * TILES, :] = orb_v[b, (4 + o) * TILES : (5 + o) * TILES].astype(F32)

    def form(group, _):
        for u in range(6):
            j = 6 * group + u
            orbs = orbf[pl.ds(j, 64, stride=TILES), :].astype(BF16)
            rows = contract(orbs, pick3[...], ((0,), (0,)))
            rhs[tile(j), :] = rows[:, 0:128] * rows[:, 128:256] * rows[:, 256:384]
        return 0

    lax.fori_loop(0, TILES // 6, form, 0)

    def weigh(group, _):
        for u in range(4):
            j = 4 * group + u
            orbs = orbf[pl.ds(j, 64, stride=TILES), :].astype(BF16)
            occ = contract(pick_occ[...], orbs, ((1,), (0,)))
            vir = contract(pick_vir[...], orbs, ((1,), (0,)))
            w_buf[:, tile(j)] = (occ * vir * quad_v[pl.ds(j, 1), :]).astype(BF16)
        return 0

    place8 = iota((8, 128), 0)

    def rows_of(source, index, row, start, count=8):
        merged = None
        for u in range(count):
            at = pl.ds(index[row, start + u], 1)
            spread = jnp.broadcast_to(source[at, :], (8, 128))
            merged = spread if u == 0 else jnp.where(place8 == u, spread, merged)
        return merged

    index_slots = (index_a, index_b)

    def index_copy(source, chunk, slot):
        rows8 = pl.ds(pl.multiple_of(chunk * 8, 8), 8)
        return pltpu.make_async_copy(
            source.at[rows8, :], index_slots[slot], index_sem.at[slot]
        )

    def permute(source, table, target, after_first):
        chunks = TILES // 8
        for slot in range(2):
            index_copy(source, slot, slot).start()

        def permute_step(i, _):
            for slot in range(2):
                index_copy(source, 0, slot).wait()
                base = pl.multiple_of((2 * i + slot) * 1024, 1024)
                for row in range(8):
                    for u in range(0, 128, 8):
                        found = rows_of(table, index_slots[slot], row, u)
                        target[pl.ds(base + 128 * row + u, 8), :] = found
                index_copy(source, lax.rem(2 * i + 2 + slot, chunks), slot).start()
            return 0

        if after_first is None:
            lax.fori_loop(0, chunks // 2, permute_step, 0)
        else:
            lax.fori_loop(0, 1, permute_step, 0)
            after_first()
            lax.fori_loop(1, chunks // 2, permute_step, 0)
        for slot in range(2):
            index_copy(source, 0, slot).wait()

    has_below = dom > 0
    has_above = dom < DOM - 1

    def face_copy(rnd, side, target):
        return pltpu.make_async_remote_copy(
            src_ref=face_send.at[rnd, 1 - side],
            dst_ref=face_recv.at[rnd, side],
            send_sem=face_ss.at[rnd, side],
            recv_sem=face_rs.at[rnd, side],
            device_id={"dom": target},
            device_id_type=MESH,
        )

    def send_faces(rnd):
        @pl.when(has_above)
        def _():
            face_copy(rnd, 0, dom + 1).start()

        @pl.when(has_below)
        def _():
            face_copy(rnd, 1, dom - 1).start()

    def add_faces(rnd, field):
        @pl.when(has_below)
        def _():
            face_copy(rnd, 0, dom - 1).wait_recv()

            def body(j, _):
                got = face_recv[rnd, 0, tile(j), :].astype(F32)
                field[tile(j), :] += got + swap(got)
                return 0

            lax.fori_loop(0, 6, body, 0)

        @pl.when(has_above)
        def _():
            face_copy(rnd, 1, dom + 1).wait_recv()

            def body(j, _):
                got = face_recv[rnd, 1, tile(j), :].astype(F32)
                field[tile(j + 6), :] += got + swap(got)
                return 0

            lax.fori_loop(0, 6, body, 0)

        @pl.when(has_above)
        def _():
            face_copy(rnd, 0, dom + 1).wait_send()

        @pl.when(has_below)
        def _():
            face_copy(rnd, 1, dom - 1).wait_send()

    def pack_faces(rnd, field):
        def body(j, _):
            for side in range(2):
                value = field[tile(j + 6 * side), :]
                face_send[rnd, side, tile(j), :] = halves(value).astype(BF16)
            return 0

        lax.fori_loop(0, 6, body, 0)

    def first_faces():
        pack_faces(0, r0)
        @pl.when(mine)
        def _():
            pl.semaphore_wait(barrier, DOM - 1 + DOM - 1)

        @pl.when(jnp.logical_not(mine))
        def _():
            pl.semaphore_wait(barrier, DOM - 1 + DOM)

        send_faces(0)

    permute(old_v, rhs, r0, first_faces)
    lax.fori_loop(0, 3, weigh, 0)
    add_faces(0, r0)

    lower_share = jnp.where(has_below, 0.5, 1.0).astype(F32)
    upper_share = jnp.where(has_above, 0.5, 1.0).astype(F32)
    zero_acc = jnp.zeros((8, 128), F32)

    ranges = ((0, 6, lower_share), (6, 12, upper_share), (12, TILES, 1.0))
    rr_part = zero_acc
    for start, stop, share in ranges:

        def start_split(j, acc):
            value = r0[tile(j), :]
            split[tile(j), :] = halves(value)
            return acc + fold(value * value)

        rr_part = rr_part + share * lax.fori_loop(start, stop, start_split, zero_acc)
    rd_part = zero_acc

    def stream(source, per_step, fetch, hold, work, finish, init):
        per_chunk = 8 // per_step
        steps = CELLS // per_step
        chunks = CELLS // 8
        for slot in range(2):
            index_copy(source, slot, slot).start()
        index_copy(source, 0, 0).wait()
        fetch(index_a, 0)

        def stream_step(i, carry):
            for m in range(2 * per_chunk):
                step = 2 * per_chunk * i + m
                slot, row = divmod((m + 1) % (2 * per_chunk), per_chunk)
                if row == 0:
                    index_copy(source, 0, slot).wait()
                carry = finish(lax.rem(step + steps - 1, steps), carry)
                held = hold()
                fetch(index_slots[slot], row * per_step)
                work(step, held)
                if row == per_chunk - 1:
                    index_copy(source, lax.rem(2 * i + 2 + slot, chunks), slot).start()
            return carry

        carry = lax.fori_loop(0, chunks // 2, stream_step, init)
        index_copy(source, 0, 1).wait()
        return finish(steps - 1, carry)

    def gather_four(index, row):
        for h in range(4):
            for u in range(0, 128, 8):
                count = min(8, NPC - u)
                ga[pl.ds(128 * h + u, 8), :] = rows_of(split, index, row + h, u, count)

    def held_four():
        high, low = [], []
        for h in range(2):
            first = ga[256 * h : 256 * h + 128, :]
            second = ga[256 * h + 128 : 256 * h + 256, :]
            high.append(jnp.where(low_half, first, swap(second)).astype(BF16))
            low.append(jnp.where(low_half, swap(first), second).astype(BF16))
        return high, low

    def cell_work(i, held):
        high, low = held
        stacked = jnp.concatenate(
            [jnp.concatenate(high, axis=1), jnp.concatenate(low, axis=1)], axis=0
        )
        product = contract(elem2[...], stacked, ((1,), (0,)))
        products[...] = product[0:128, :] + product[128:256, :]
        for h in range(2):
            whole[:, 128 * h : 128 * h + 128] = high[h].astype(F32) + low[h].astype(F32)

    def cells(keep_rows):
        products[...] = jnp.zeros((128, 256), F32)
        whole[...] = jnp.zeros((128, 256), F32)

        def cell_finish(i, acc):
            for h in range(2):
                cell = 4 * i + 2 * h
                at = slice(128 * h, 128 * h + 128)
                rows = products[:, at] * jnp.where(low_half, coef_s[cell], coef_s[cell + 1])
                acc = acc + fold(whole[:, at] * rows)
                if keep_rows:
                    turned = swap(rows)
                    y_buf[tile(cell), :] = halves(jnp.where(low_half, rows, turned))
                    y_buf[tile(cell + 1), :] = halves(jnp.where(low_half, turned, rows))
            return acc

        return stream(node_v, 4, gather_four, held_four, cell_work, cell_finish, zero_acc)

    def one_row(value):
        return jnp.sum(value, axis=0, keepdims=True)

    def send_dots(rnd, rows):
        packed = jnp.concatenate(rows + [jnp.zeros((8 - len(rows), 128), F32)], axis=0)
        dot_send[rnd] = packed
        dot_recv[rnd, dom] = packed
        for off in range(1, DOM):
            pltpu.make_async_remote_copy(
                src_ref=dot_send.at[rnd],
                dst_ref=dot_recv.at[rnd, dom],
                send_sem=dot_ss.at[rnd, off],
                recv_sem=dot_rs.at[rnd, dom],
                device_id={"dom": lax.rem(dom + off, DOM)},
                device_id_type=MESH,
            ).start()

    def sum_dots(rnd):
        for off in range(1, DOM):
            source = lax.rem(dom + off, DOM)
            copy = pltpu.make_async_remote_copy(
                src_ref=dot_send.at[rnd],
                dst_ref=dot_recv.at[rnd, source],
                send_sem=dot_ss.at[rnd, off],
                recv_sem=dot_rs.at[rnd, source],
                device_id={"dom": source},
                device_id_type=MESH,
            )
            copy.wait_recv()
            copy.wait_send()
        total = jnp.sum(dot_recv[rnd], axis=0)
        return [total[k : k + 1, :] for k in range(3)]

    def gather_entries(index, row):
        for h in range(2):
            for u in range(0, 128, 8):
                gx[pl.ds(128 * h + u, 8), :] = rows_of(y_buf, index, row + h, u)

    node_rows = iota((64 * WINDOW, 256), 0)

    def entry_work(t, held):
        ids = [sid_v[pl.ds(2 * t + h, 1), :] for h in range(2)]
        ids = jnp.concatenate(ids, axis=1) - walk_s[0, t] * 64
        hot = jnp.where(ids == node_rows, 1.0, 0.0).astype(BF16)
        terms[...] = contract(hot, held, ((1,), (0,)))

    def entry_finish(t, carry):
        moved = walk_s[1, t]
        now = [window[moved + k] + terms[64 * k : 64 * k + 64, :] for k in range(WINDOW)]
        for k in range(WINDOW):
            window[k] = now[k]
            sums[t, k] = now[k]
        return carry

    def sum_entries():
        window[...] = jnp.zeros((2 * WINDOW - 1, 64, 128), F32)
        terms[...] = jnp.zeros((64 * WINDOW, 128), F32)

        def hold():
            return gx[...].astype(BF16)

        stream(perm_v, 2, gather_entries, hold, entry_work, entry_finish, 0)

    def take(j):
        parts = [sums[walk_s[2, 2 * j + h], walk_s[3, 2 * j + h]] for h in range(2)]
        value = jnp.concatenate(parts, axis=0)
        return value + swap(value)

    old_rr = old_den = beta = None
    fields = (r0, r1, r2)
    steps = []
    for it in range(2):
        now, later = fields[it], fields[it + 1]
        quad_part = one_row(cells(True))
        send_dots(it + 1, [one_row(rr_part), one_row(rd_part), quad_part + swap(quad_part)])
        sum_entries()

        def set_faces(j, _):
            value = take(j)
            zf[tile(j), :] = value
            return 0

        lax.fori_loop(0, 12, set_faces, 0)
        pack_faces(it + 1, zf)
        send_faces(it + 1)
        lax.fori_loop(3 * it + 3, 3 * it + 6, weigh, 0)
        rr, rd, quad_form = sum_dots(it + 1)
        if it == 0:
            den = quad_form
        else:
            beta = rr / old_rr
            den = quad_form + 2.0 * beta * rd + beta * beta * old_den
        alpha = rr / den
        steps.append((alpha, beta))

        def advance(j, value, accs, it=it, now=now, later=later, alpha=alpha, beta=beta):
            image = value
            if it == 0:
                im0[tile(j), :] = image
            else:
                image = image + beta * im0[tile(j), :]
            new = now[tile(j), :] - alpha * image
            later[tile(j), :] = new
            split[tile(j), :] = halves(new)
            return accs[0] + fold(new * new), accs[1] + fold(new * image)

        none = (zero_acc, zero_acc)

        def inner(group, accs):
            for u in range(3):
                j = 3 * group + u
                accs = advance(j, take(j), accs)
            return accs

        rr_part, rd_part = lax.fori_loop(4, TILES // 3, inner, none)
        add_faces(it + 1, zf)
        for start, stop, share in ranges[:2]:

            def outer(group, accs):
                for u in range(3):
                    j = 3 * group + u
                    accs = advance(j, zf[tile(j), :], accs)
                return accs

            more = lax.fori_loop(start // 3, stop // 3, outer, none)
            rr_part = rr_part + share * more[0]
            rd_part = rd_part + share * more[1]
        old_rr, old_den = rr, den

    quad_part = one_row(cells(False))
    send_dots(3, [one_row(rr_part), one_row(rd_part), quad_part + swap(quad_part)])
    lax.fori_loop(9, 12, weigh, 0)
    rr, rd, quad_form = sum_dots(3)
    last_beta = rr / old_rr
    den = quad_form + 2.0 * last_beta * rd + last_beta * last_beta * old_den
    scale2 = rr / den
    scale1 = steps[1][0] + scale2 * last_beta
    scale0 = steps[0][0] + scale1 * steps[1][1]

    def combine(j, _):
        at = tile(j)
        split[at, :] = scale0 * r0[at, :] + scale1 * r1[at, :] + scale2 * r2[at, :]
        return 0

    lax.fori_loop(0, TILES, combine, 0)

    permute(new_v, split, rhs, None)

    c_acc[...] = jnp.zeros((PAIRS, 128), F32)

    def couple(k, _):
        at = pl.ds(pl.multiple_of(k * 512, 512), 512)
        c_acc[...] += contract(w_buf[:, at], rhs[at, :].astype(BF16), ((1,), (0,)))
        return 0

    lax.fori_loop(0, NODES // 512, couple, 0)

    def c_copy(piece, slot, device):
        return pltpu.make_async_remote_copy(
            src_ref=c_send.at[piece],
            dst_ref=c_recv.at[slot],
            send_sem=c_ss.at[piece],
            recv_sem=c_rs.at[slot],
            device_id=device,
            device_id_type=MESH,
        )

    for b in range(BAND):
        block = c_acc[OWN * b : OWN * b + OWN, :]
        turned = jnp.concatenate([block, block], axis=0).T
        for h in range(2):
            piece = 2 * b + h
            upper = turned[32 * h : 32 * h + 16, :]
            lower = turned[32 * h + 16 : 32 * h + 32, :]
            c_send[piece] = jnp.where(low_half[0:16, :], upper, lower)
            to_self = jnp.logical_and(band == b, dom == 2 * band + h)

            @pl.when(jnp.logical_not(to_self))
            def _(b=b, h=h, piece=piece):
                c_copy(piece, dom, {"band": b, "dom": 2 * band + h}).start()

            @pl.when(to_self)
            def _(piece=piece):
                c_recv[dom] = c_send[piece]

    def deliver(group, _):
        for u in range(4):
            j = 4 * group + u
            pot_out[:, tile(j)] = rhs[tile(j), :].T[0:OWN, :]
        return 0

    lax.fori_loop(0, TILES // 4, deliver, 0)

    for off in range(DOM):
        source = lax.rem(dom + off, DOM)
        from_self = jnp.logical_and(mine, source == dom)

        @pl.when(jnp.logical_not(from_self))
        def _(source=source):
            c_copy(0, source, {"band": half_dom, "dom": source}).wait_recv()

    total = jnp.sum(c_recv[...], axis=0) * (1.0 / (NODES * DOM))
    coup_out[...] = jnp.concatenate([total, swap(total)], axis=0)[:, 0:OWN]

    for b in range(BAND):
        for h in range(2):
            piece = 2 * b + h
            to_self = jnp.logical_and(band == b, dom == 2 * band + h)

            @pl.when(jnp.logical_not(to_self))
            def _(b=b, h=h, piece=piece):
                c_copy(piece, dom, {"band": b, "dom": 2 * band + h}).wait_send()


def on_device(
    occ_orb, vir_orb, pair_list, quad_weight, cell_coef, connect, face_map, element_matrix
):
    index = build_index(connect, face_map, occ_orb, vir_orb)
    node, ordered, perm, walk, new, old, orbs = index
    quad = quad_weight.reshape(TILES, 128)
    vmem = pl.BlockSpec(memory_space=pltpu.VMEM)
    smem = pl.BlockSpec(memory_space=pltpu.SMEM)
    dma = pltpu.SemaphoreType.DMA
    field = pltpu.VMEM((NODES, 128), F32)
    potential, coupling = pl.pallas_call(
        main_kernel,
        out_shape=(
            jax.ShapeDtypeStruct((OWN, NODES), F32),
            jax.ShapeDtypeStruct((32, OWN), F32),
        ),
        in_specs=[smem] * 2 + [vmem] * 9,
        out_specs=(vmem, vmem),
        scratch_shapes=[
            pltpu.VMEM((64 * TILES, 128), F32),
            pltpu.VMEM((64, 384), BF16),
            pltpu.VMEM((PAIRS, 64), BF16),
            pltpu.VMEM((PAIRS, 64), BF16),
            pltpu.VMEM((256, 256), BF16),
            field, field, field, field, field, field,
            pltpu.VMEM((CELLS * 128, 128), F32),
            pltpu.VMEM((256, 128), F32),
            pltpu.VMEM((2 * WINDOW - 1, 64, 128), F32),
            pltpu.VMEM((ENTRY_TILES, WINDOW, 64, 128), F32),
            pltpu.VMEM((64 * WINDOW, 128), F32),
            pltpu.VMEM((128, 256), F32),
            pltpu.VMEM((128, 256), F32),
            pltpu.VMEM((PAIRS, NODES), BF16),
            pltpu.VMEM((512, 128), F32),
            pltpu.VMEM((2 * FACE, 128), F32),
            pltpu.VMEM((PAIRS, 128), F32),
            pltpu.VMEM((CELLS, 128), I32),
            pltpu.SMEM((8, 128), I32),
            pltpu.SMEM((8, 128), I32),
            pltpu.VMEM((3, 2, FACE, 128), BF16),
            pltpu.VMEM((3, 2, FACE, 128), BF16),
            pltpu.VMEM((4, 8, 128), F32),
            pltpu.VMEM((4, DOM, 8, 128), F32),
            pltpu.VMEM((DOM, 16, 128), F32),
            pltpu.VMEM((DOM, 16, 128), F32),
            dma((3, 2)),
            dma((3, 2)),
            dma((4, DOM)),
            dma((4, DOM)),
            dma((DOM,)),
            dma((DOM,)),
            dma((2,)),
        ],
        compiler_params=pltpu.CompilerParams(
            collective_id=0, has_side_effects=True, vmem_limit_bytes=60 * 1024 * 1024
        ),
        name="solve",
    )(walk, cell_coef, new, old, node, perm, ordered, orbs, quad, pair_list, element_matrix)
    return potential, coupling.T


def solution(mesh):
    return jax.shard_map(
        on_device,
        mesh=mesh,
        in_specs=(
            P("band", "dom"),
            P("band", "dom"),
            P(),
            P("dom"),
            P("dom"),
            P(None, "dom"),
            P(None, "dom"),
            P(),
        ),
        out_specs=(P("band", "dom"), P("band", "dom")),
        check_vma=False,
    )
```

```python
import jax
import jax.numpy as jnp
from jax import lax
from jax.experimental import pallas as pl
from jax.experimental.pallas import tpu as pltpu
from jax.sharding import PartitionSpec as P

NODES = 6144
TILES = 48
CELLS = 96
NPC = 125
FACE = 768
BAND = 8
DOM = 16
PAIRS = 512
OWN = 64
ENTRY_TILES = 48
WINDOW = 5
F32 = jnp.float32
BF16 = jnp.bfloat16
I32 = jnp.int32
MESH = pl.DeviceIdType.MESH


def iota(shape, dim):
    return lax.broadcasted_iota(I32, shape, dim)


def contract(first, second, dims):
    return lax.dot_general(first, second, (dims, ((), ())), preferred_element_type=F32)


def index_kernel(
    conn_ref, face_ref, occ_ref, vir_ref,
    key_ref, node_ref, new_ref, old_ref, orb_ref,
    turn, orb_rows, orb_own, orb_all, orb_ss, orb_rs,
):
    band = lax.axis_index("band")
    barrier = pltpu.get_barrier_semaphore()
    for off in range(1, BAND):
        pl.semaphore_signal(
            barrier, 1, device_id={"band": lax.rem(band + off, BAND)}, device_id_type=MESH
        )
    occ = occ_ref[...].astype(F32)
    vir = vir_ref[...].astype(F32)
    for j in range(TILES):
        at = slice(128 * j, 128 * j + 128)
        orb_rows[pl.ds(j, 4, stride=TILES), :] = occ[:, at]
        orb_rows[pl.ds(4 * TILES + j, 2, stride=TILES), :] = vir[:, at]
    orb_own[...] = orb_rows[0 : 6 * TILES, :].astype(BF16)
    pl.semaphore_wait(barrier, BAND - 1)

    def orb_copy(off, slot, device):
        return pltpu.make_async_remote_copy(
            src_ref=orb_own,
            dst_ref=orb_all.at[slot],
            send_sem=orb_ss.at[off],
            recv_sem=orb_rs.at[slot],
            device_id={"band": device},
            device_id_type=MESH,
        )

    for off in range(1, BAND):
        orb_copy(off, band, lax.rem(band + off, BAND)).start()
    orb_all[band] = orb_own[...]

    rows48 = iota((TILES, 128), 0)
    rows128 = iota((128, 128), 0)
    lane_row = iota((1, 128), 1)

    def table(numbers, base, hit, low):
        high_hot = jnp.where(lax.shift_right_logical(numbers, 7) == rows48, 1.0, 0.0).astype(BF16)
        same = (numbers & 127) == rows128
        low_hot = jnp.where(same, 1.0, 0.0).astype(BF16)
        low_value = jnp.where(same, lane_row, 0).astype(F32).astype(BF16)
        hits = contract(high_hot, low_hot, ((1,), (1,)))
        values = contract(high_hot, low_value, ((1,), (1,)))
        return hit + hits, low + values + base * hits

    turn[...] = jnp.zeros((CELLS, 128), I32)
    turn[:, 0:NPC] = conn_ref[...]
    shared = jnp.zeros((TILES, 128), F32)
    face_id = jnp.zeros((TILES, 128), F32)
    faces = [face_ref[k : k + 1, 128 * j : 128 * j + 128] for k in range(2) for j in range(6)]
    for j in range(2 * FACE // 128):
        shared, face_id = table(faces[j], 128.0 * j, shared, face_id)
    inner = 1.0 - shared
    inner16 = inner.astype(BF16)
    before = jnp.where(iota((128, 128), 0) < iota((128, 128), 1), 1.0, 0.0).astype(BF16)
    above = jnp.where(iota((TILES, TILES), 1) < iota((TILES, TILES), 0), 1.0, 0.0).astype(BF16)
    in_row = contract(inner16, before, ((1,), (0,)))
    rows_above = jnp.sum(contract(above, inner16, ((1,), (0,))), axis=1, keepdims=True)
    number = jnp.where(shared > 0.5, face_id, in_row + rows_above + 2.0 * FACE)
    new_ref[...] = number.astype(I32)

    def invert(group, carry):
        hit, low = carry
        for u in range(8):
            base = (1024 * group + 128 * u).astype(F32)
            hit, low = table(new_ref[pl.ds(8 * group + u, 1), :], base, hit, low)
        return hit, low

    zero = jnp.zeros((TILES, 128), F32)
    _, old = lax.fori_loop(0, TILES // 8, invert, (zero, zero))
    old_ref[...] = old.astype(I32)

    number_int = number.astype(I32)
    high_part = lax.shift_right_logical(number_int, 7).astype(F32)
    low_part = (number_int & 127).astype(F32)
    parts = jnp.concatenate([high_part, low_part], axis=1).T.astype(BF16)

    def look_up(group, _):
        found = []
        for u in range(8):
            nodes = turn[pl.ds(group * 8 + u, 1), :]
            hot = jnp.where(lax.shift_right_logical(nodes, 7) == rows48, 1.0, 0.0).astype(BF16)
            both = contract(parts, hot, ((1,), (0,)))
            value = 128.0 * both[:128] + both[128:]
            same = (nodes & 127) == rows128
            found.append(jnp.sum(jnp.where(same, value, 0.0), axis=0, keepdims=True))
        ids = jnp.concatenate(found, axis=0).astype(I32)
        lanes = iota((8, 128), 1)
        code = (iota((8, 128), 0) + group * 8) * 128 + lanes
        real = lanes < NPC
        at = pl.ds(pl.multiple_of(group * 8, 8), 8)
        key_ref[at, :] = jnp.where(real, ids, NODES) * 16384 + code
        node_ref[at, :] = jnp.where(real, ids, 0)
        return 0

    lax.fori_loop(0, CELLS // 8, look_up, 0)
    for off in range(1, BAND):
        source = lax.rem(band + off, BAND)
        orb_copy(off, source, source).wait_recv()
    orb_ref[...] = orb_all[...]
    for off in range(1, BAND):
        orb_copy(off, band, lax.rem(band + off, BAND)).wait_send()


def build_index(connect, face_map, occ_orb, vir_orb):
    vmem = pl.BlockSpec(memory_space=pltpu.VMEM)
    shape = jax.ShapeDtypeStruct
    dma = pltpu.SemaphoreType.DMA
    key, node, new, old, orbs = pl.pallas_call(
        index_kernel,
        out_shape=[
            shape((CELLS, 128), I32),
            shape((CELLS, 128), I32),
            shape((TILES, 128), I32),
            shape((TILES, 128), I32),
            shape((BAND, 6 * TILES, 128), BF16),
        ],
        in_specs=[vmem] * 4,
        out_specs=[vmem] * 5,
        scratch_shapes=[
            pltpu.VMEM((CELLS, 128), I32),
            pltpu.VMEM((12 * TILES, 128), F32),
            pltpu.VMEM((6 * TILES, 128), BF16),
            pltpu.VMEM((BAND, 6 * TILES, 128), BF16),
            dma((BAND,)),
            dma((BAND,)),
        ],
        compiler_params=pltpu.CompilerParams(
            collective_id=1, has_side_effects=True, vmem_limit_bytes=60 * 1024 * 1024
        ),
        name="index",
    )(connect.T, face_map, occ_orb, vir_orb)
    ordered = lax.sort(key.reshape(CELLS * 128), is_stable=False).reshape(CELLS, 128)
    block = lax.shift_right_logical(ordered[0:94:2, 0], 20)
    place = jnp.arange(128, dtype=I32)
    begins = block[None, :] <= place[:, None]
    last_tile = jnp.sum(begins.astype(I32), axis=1) - 1
    last_block = jnp.max(jnp.where(begins, block[None, :], 0), axis=1)
    within = jnp.clip(place - last_block, 0, WINDOW - 1)
    move = jnp.clip(block[1:] - block[:-1], 0, WINDOW - 1)
    walk = jnp.stack(
        [jnp.pad(block, (0, 81)), jnp.pad(move, (1, 81)), jnp.clip(last_tile, 0, 46), within]
    )
    return node, ordered, ordered & 16383, walk, new, old, orbs


def main_kernel(
    walk_s, coef_s,
    new_v, old_v, node_v, perm_v, ordered_v, orb_v, quad_v, pairs_v, elem_v,
    pot_out, coup_out,
    orbf, pick3, pick_occ, pick_vir, elem2,
    rhs, r0, r1, r2, im0, split, y_buf, gx, window, sums, terms, products, whole, w_buf, ga, zf, c_acc, sid_v, index_a, index_b,
    face_send, face_recv, dot_send, dot_recv, c_send, c_recv,
    face_ss, face_rs, dot_ss, dot_rs, c_ss, c_rs, index_sem,
):
    dom = lax.axis_index("dom")
    band = lax.axis_index("band")
    half_dom = lax.div(dom, 2)
    low_half = iota((128, 128), 1) < 64

    def swap(value):
        return pltpu.roll(value, 64, 1)

    def halves(value):
        high = value.astype(BF16).astype(F32)
        return jnp.where(low_half, high, value - high)

    def tile(j):
        return pl.ds(pl.multiple_of(j * 128, 128), 128)

    def fold(value):
        return jnp.sum(value.reshape(16, 8, 128), axis=0)

    barrier = pltpu.get_barrier_semaphore()
    for off in range(1, DOM):
        pl.semaphore_signal(
            barrier, 1, device_id={"dom": lax.rem(dom + off, DOM)}, device_id_type=MESH
        )
    mine = half_dom == band
    for off in range(DOM):
        source = lax.rem(dom + off, DOM)

        @pl.when(jnp.logical_not(jnp.logical_and(mine, source == dom)))
        def _():
            pl.semaphore_signal(
                barrier, 1, device_id={"band": half_dom, "dom": source}, device_id_type=MESH
            )

    sid_v[...] = lax.shift_right_logical(ordered_v[...], 14)

    occ_of = pairs_v[0:1, :]
    vir_of = pairs_v[1:2, :]
    orbital = iota((64, PAIRS), 0)
    occ_hot = jnp.where(orbital == occ_of, 1.0, 0.0)
    vir_hot = jnp.where(orbital == vir_of + 32, 1.0, 0.0)
    pick_occ[...] = occ_hot.T.astype(BF16)
    pick_vir[...] = vir_hot.T.astype(BF16)
    own = (iota((PAIRS, 128), 1) & 63) + band * OWN == iota((PAIRS, 128), 0)
    own = jnp.where(own, 1.0, 0.0).astype(BF16)
    pick3[:, 0:128] = contract(occ_hot.astype(BF16), own, ((1,), (0,))).astype(BF16)
    pick3[:, 128:256] = contract(vir_hot.astype(BF16), own, ((1,), (0,))).astype(BF16)
    weight_row = iota((64, 128), 0)
    weight_row = jnp.logical_and(weight_row >= 48, weight_row < 51)
    pick3[:, 256:384] = jnp.where(weight_row, 1.0, 0.0).astype(BF16)
    ga[0:128, :] = jnp.zeros((128, 128), F32)
    ga[0:NPC, 0:NPC] = elem_v[...]
    elem = ga[0:128, :]
    elem_high = elem.astype(BF16)
    elem_low = (elem - elem_high.astype(F32)).astype(BF16)
    elem2[...] = jnp.concatenate(
        [
            jnp.concatenate([elem_high, elem_high], axis=1),
            jnp.concatenate([elem_low, elem_low], axis=1),
        ],
        axis=0,
    )
    quad = quad_v[...]
    quad_high = quad.astype(BF16).astype(F32)
    quad_rest = quad - quad_high
    quad_mid = quad_rest.astype(BF16).astype(F32)
    orbf[48 * TILES : 49 * TILES, :] = quad_high
    orbf[49 * TILES : 50 * TILES, :] = quad_mid
    orbf[50 * TILES : 51 * TILES, :] = quad_rest - quad_mid
    orbf[51 * TILES : 64 * TILES, :] = jnp.zeros((13 * TILES, 128), F32)
    ga[120:128, :] = jnp.zeros((8, 128), F32)
    ga[248:256, :] = jnp.zeros((8, 128), F32)
    ga[376:384, :] = jnp.zeros((8, 128), F32)
    ga[504:512, :] = jnp.zeros((8, 128), F32)

    for b in range(BAND):
        for o in range(4):
            orbf[(4 * b + o) * TILES : (4 * b + o + 1) * TILES, :] = orb_v[b, o * TILES : (o + 1) * TILES].astype(F32)
        for o in range(2):
            at = 32 + 2 * b + o
            orbf[at * TILES : (at + 1) * TILES, :] = orb_v[b, (4 + o) * TILES : (5 + o) * TILES].astype(F32)

    def form(group, _):
        for u in range(6):
            j = 6 * group + u
            orbs = orbf[pl.ds(j, 64, stride=TILES), :].astype(BF16)
            rows = contract(orbs, pick3[...], ((0,), (0,)))
            rhs[tile(j), :] = rows[:, 0:128] * rows[:, 128:256] * rows[:, 256:384]
        return 0

    lax.fori_loop(0, TILES // 6, form, 0)

    def weigh(group, _):
        for u in range(4):
            j = 4 * group + u
            orbs = orbf[pl.ds(j, 64, stride=TILES), :].astype(BF16)
            occ = contract(pick_occ[...], orbs, ((1,), (0,)))
            vir = contract(pick_vir[...], orbs, ((1,), (0,)))
            w_buf[:, tile(j)] = (occ * vir * quad_v[pl.ds(j, 1), :]).astype(BF16)
        return 0

    place8 = iota((8, 128), 0)

    def rows_of(source, index, row, start, count=8):
        merged = None
        for u in range(count):
            at = pl.ds(index[row, start + u], 1)
            spread = jnp.broadcast_to(source[at, :], (8, 128))
            merged = spread if u == 0 else jnp.where(place8 == u, spread, merged)
        return merged

    index_slots = (index_a, index_b)

    def index_copy(source, chunk, slot):
        rows8 = pl.ds(pl.multiple_of(chunk * 8, 8), 8)
        return pltpu.make_async_copy(
            source.at[rows8, :], index_slots[slot], index_sem.at[slot]
        )

    def permute(source, table, target, after_first):
        chunks = TILES // 8
        for slot in range(2):
            index_copy(source, slot, slot).start()

        def permute_step(i, _):
            for slot in range(2):
                index_copy(source, 0, slot).wait()
                base = pl.multiple_of((2 * i + slot) * 1024, 1024)
                for row in range(8):
                    for u in range(0, 128, 8):
                        found = rows_of(table, index_slots[slot], row, u)
                        target[pl.ds(base + 128 * row + u, 8), :] = found
                index_copy(source, lax.rem(2 * i + 2 + slot, chunks), slot).start()
            return 0

        if after_first is None:
            lax.fori_loop(0, chunks // 2, permute_step, 0)
        else:
            lax.fori_loop(0, 1, permute_step, 0)
            after_first()
            lax.fori_loop(1, chunks // 2, permute_step, 0)
        for slot in range(2):
            index_copy(source, 0, slot).wait()

    has_below = dom > 0
    has_above = dom < DOM - 1

    def face_copy(rnd, side, target):
        return pltpu.make_async_remote_copy(
            src_ref=face_send.at[rnd, 1 - side],
            dst_ref=face_recv.at[rnd, side],
            send_sem=face_ss.at[rnd, side],
            recv_sem=face_rs.at[rnd, side],
            device_id={"dom": target},
            device_id_type=MESH,
        )

    def send_faces(rnd):
        @pl.when(has_above)
        def _():
            face_copy(rnd, 0, dom + 1).start()

        @pl.when(has_below)
        def _():
            face_copy(rnd, 1, dom - 1).start()

    def add_faces(rnd, field):
        @pl.when(has_below)
        def _():
            face_copy(rnd, 0, dom - 1).wait_recv()

            def body(j, _):
                for u in range(3):
                    got = face_recv[rnd, 0, tile(3 * j + u), :].astype(F32)
                    field[tile(3 * j + u), :] += got + swap(got)
                return 0

            lax.fori_loop(0, 2, body, 0)

        @pl.when(has_above)
        def _():
            face_copy(rnd, 1, dom + 1).wait_recv()

            def body(j, _):
                for u in range(3):
                    got = face_recv[rnd, 1, tile(3 * j + u), :].astype(F32)
                    field[tile(3 * j + u + 6), :] += got + swap(got)
                return 0

            lax.fori_loop(0, 2, body, 0)

        @pl.when(has_above)
        def _():
            face_copy(rnd, 0, dom + 1).wait_send()

        @pl.when(has_below)
        def _():
            face_copy(rnd, 1, dom - 1).wait_send()

    def pack_faces(rnd, field):
        def body(j, _):
            for side in range(2):
                for u in range(3):
                    value = field[tile(3 * j + u + 6 * side), :]
                    face_send[rnd, side, tile(3 * j + u), :] = halves(value).astype(BF16)
            return 0

        lax.fori_loop(0, 2, body, 0)

    def first_faces():
        pack_faces(0, r0)
        @pl.when(mine)
        def _():
            pl.semaphore_wait(barrier, DOM - 1 + DOM - 1)

        @pl.when(jnp.logical_not(mine))
        def _():
            pl.semaphore_wait(barrier, DOM - 1 + DOM)

        send_faces(0)

    permute(old_v, rhs, r0, first_faces)
    lax.fori_loop(0, 3, weigh, 0)
    add_faces(0, r0)

    lower_share = jnp.where(has_below, 0.5, 1.0).astype(F32)
    upper_share = jnp.where(has_above, 0.5, 1.0).astype(F32)
    zero_acc = jnp.zeros((8, 128), F32)

    ranges = ((0, 6, lower_share), (6, 12, upper_share), (12, TILES, 1.0))
    rr_part = zero_acc
    for start, stop, share in ranges:

        def start_split(group, acc):
            for u in range(3):
                value = r0[tile(3 * group + u), :]
                split[tile(3 * group + u), :] = halves(value)
                acc = acc + fold(value * value)
            return acc

        rr_part = rr_part + share * lax.fori_loop(start // 3, stop // 3, start_split, zero_acc)
    rd_part = zero_acc

    def stream(source, per_step, fetch, hold, work, finish, init):
        per_chunk = 8 // per_step
        steps = CELLS // per_step
        chunks = CELLS // 8
        for slot in range(2):
            index_copy(source, slot, slot).start()
        index_copy(source, 0, 0).wait()
        fetch(index_a, 0)

        def stream_step(i, carry):
            for m in range(2 * per_chunk):
                step = 2 * per_chunk * i + m
                slot, row = divmod((m + 1) % (2 * per_chunk), per_chunk)
                if row == 0:
                    index_copy(source, 0, slot).wait()
                carry = finish(lax.rem(step + steps - 1, steps), carry)
                held = hold()
                fetch(index_slots[slot], row * per_step)
                work(step, held)
                if row == per_chunk - 1:
                    index_copy(source, lax.rem(2 * i + 2 + slot, chunks), slot).start()
            return carry

        carry = lax.fori_loop(0, chunks // 2, stream_step, init)
        index_copy(source, 0, 1).wait()
        return finish(steps - 1, carry)

    def gather_four(index, row):
        for h in range(4):
            for u in range(0, 128, 8):
                count = min(8, NPC - u)
                ga[pl.ds(128 * h + u, 8), :] = rows_of(split, index, row + h, u, count)

    def held_four():
        high, low = [], []
        for h in range(2):
            first = ga[256 * h : 256 * h + 128, :]
            second = ga[256 * h + 128 : 256 * h + 256, :]
            high.append(jnp.where(low_half, first, swap(second)).astype(BF16))
            low.append(jnp.where(low_half, swap(first), second).astype(BF16))
        return high, low

    def cell_work(i, held):
        high, low = held
        stacked = jnp.concatenate(
            [jnp.concatenate(high, axis=1), jnp.concatenate(low, axis=1)], axis=0
        )
        product = contract(elem2[...], stacked, ((1,), (0,)))
        products[...] = product[0:128, :] + product[128:256, :]
        for h in range(2):
            whole[:, 128 * h : 128 * h + 128] = high[h].astype(F32) + low[h].astype(F32)

    def cells(keep_rows):
        products[...] = jnp.zeros((128, 256), F32)
        whole[...] = jnp.zeros((128, 256), F32)

        def cell_finish(i, acc):
            for h in range(2):
                cell = 4 * i + 2 * h
                at = slice(128 * h, 128 * h + 128)
                rows = products[:, at] * jnp.where(low_half, coef_s[cell], coef_s[cell + 1])
                acc = acc + fold(whole[:, at] * rows)
                if keep_rows:
                    turned = swap(rows)
                    y_buf[tile(cell), :] = halves(jnp.where(low_half, rows, turned))
                    y_buf[tile(cell + 1), :] = halves(jnp.where(low_half, turned, rows))
            return acc

        return stream(node_v, 4, gather_four, held_four, cell_work, cell_finish, zero_acc)

    def one_row(value):
        return jnp.sum(value, axis=0, keepdims=True)

    def send_dots(rnd, rows):
        packed = jnp.concatenate(rows + [jnp.zeros((8 - len(rows), 128), F32)], axis=0)
        dot_send[rnd] = packed
        dot_recv[rnd, dom] = packed
        for off in range(1, DOM):
            pltpu.make_async_remote_copy(
                src_ref=dot_send.at[rnd],
                dst_ref=dot_recv.at[rnd, dom],
                send_sem=dot_ss.at[rnd, off],
                recv_sem=dot_rs.at[rnd, dom],
                device_id={"dom": lax.rem(dom + off, DOM)},
                device_id_type=MESH,
            ).start()

    def sum_dots(rnd):
        for off in range(1, DOM):
            source = lax.rem(dom + off, DOM)
            copy = pltpu.make_async_remote_copy(
                src_ref=dot_send.at[rnd],
                dst_ref=dot_recv.at[rnd, source],
                send_sem=dot_ss.at[rnd, off],
                recv_sem=dot_rs.at[rnd, source],
                device_id={"dom": source},
                device_id_type=MESH,
            )
            copy.wait_recv()
            copy.wait_send()
        total = jnp.sum(dot_recv[rnd], axis=0)
        return [total[k : k + 1, :] for k in range(3)]

    def gather_entries(index, row):
        for h in range(2):
            for u in range(0, 128, 8):
                gx[pl.ds(128 * h + u, 8), :] = rows_of(y_buf, index, row + h, u)

    node_rows = iota((64 * WINDOW, 256), 0)

    def entry_work(t, held):
        ids = [sid_v[pl.ds(2 * t + h, 1), :] for h in range(2)]
        ids = jnp.concatenate(ids, axis=1) - walk_s[0, t] * 64
        hot = jnp.where(ids == node_rows, 1.0, 0.0).astype(BF16)
        terms[...] = contract(hot, held, ((1,), (0,)))

    def entry_finish(t, carry):
        moved = walk_s[1, t]
        now = [window[moved + k] + terms[64 * k : 64 * k + 64, :] for k in range(WINDOW)]
        for k in range(WINDOW):
            window[k] = now[k]
            sums[t, k] = now[k]
        return carry

    def sum_entries():
        window[...] = jnp.zeros((2 * WINDOW - 1, 64, 128), F32)
        terms[...] = jnp.zeros((64 * WINDOW, 128), F32)

        def hold():
            return gx[...].astype(BF16)

        stream(perm_v, 2, gather_entries, hold, entry_work, entry_finish, 0)

    def take(j):
        parts = [sums[walk_s[2, 2 * j + h], walk_s[3, 2 * j + h]] for h in range(2)]
        value = jnp.concatenate(parts, axis=0)
        return value + swap(value)

    old_rr = old_den = beta = None
    fields = (r0, r1, r2)
    steps = []
    for it in range(2):
        now, later = fields[it], fields[it + 1]
        quad_part = one_row(cells(True))
        send_dots(it + 1, [one_row(rr_part), one_row(rd_part), quad_part + swap(quad_part)])
        sum_entries()

        def set_faces(group, _, it=it):
            for side in range(2):
                for u in range(3):
                    j = 3 * group + u
                    value = take(j + 6 * side)
                    zf[tile(j + 6 * side), :] = value
                    face_send[it + 1, side, tile(j), :] = halves(value).astype(BF16)
            return 0

        lax.fori_loop(0, 2, set_faces, 0)
        send_faces(it + 1)
        lax.fori_loop(3 * it + 3, 3 * it + 6, weigh, 0)
        rr, rd, quad_form = sum_dots(it + 1)
        if it == 0:
            den = quad_form
        else:
            beta = rr / old_rr
            den = quad_form + 2.0 * beta * rd + beta * beta * old_den
        alpha = rr / den
        steps.append((alpha, beta))

        def advance(j, value, accs, it=it, now=now, later=later, alpha=alpha, beta=beta):
            image = value
            if it == 0:
                im0[tile(j), :] = image
            else:
                image = image + beta * im0[tile(j), :]
            new = now[tile(j), :] - alpha * image
            later[tile(j), :] = new
            split[tile(j), :] = halves(new)
            return accs[0] + fold(new * new), accs[1] + fold(new * image)

        none = (zero_acc, zero_acc)

        def inner(group, accs):
            for u in range(3):
                j = 3 * group + u
                accs = advance(j, take(j), accs)
            return accs

        rr_part, rd_part = lax.fori_loop(4, TILES // 3, inner, none)
        add_faces(it + 1, zf)
        for start, stop, share in ranges[:2]:

            def outer(group, accs):
                for u in range(3):
                    j = 3 * group + u
                    accs = advance(j, zf[tile(j), :], accs)
                return accs

            more = lax.fori_loop(start // 3, stop // 3, outer, none)
            rr_part = rr_part + share * more[0]
            rd_part = rd_part + share * more[1]
        old_rr, old_den = rr, den

    quad_part = one_row(cells(False))
    send_dots(3, [one_row(rr_part), one_row(rd_part), quad_part + swap(quad_part)])
    lax.fori_loop(9, 12, weigh, 0)
    rr, rd, quad_form = sum_dots(3)
    last_beta = rr / old_rr
    den = quad_form + 2.0 * last_beta * rd + last_beta * last_beta * old_den
    scale2 = rr / den
    scale1 = steps[1][0] + scale2 * last_beta
    scale0 = steps[0][0] + scale1 * steps[1][1]

    def combine(group, _):
        for u in range(4):
            at = tile(4 * group + u)
            split[at, :] = scale0 * r0[at, :] + scale1 * r1[at, :] + scale2 * r2[at, :]
        return 0

    lax.fori_loop(0, TILES // 4, combine, 0)

    permute(new_v, split, rhs, None)

    c_acc[...] = jnp.zeros((PAIRS, 128), F32)

    def couple(k, _):
        at = pl.ds(pl.multiple_of(k * 512, 512), 512)
        c_acc[...] += contract(w_buf[:, at], rhs[at, :].astype(BF16), ((1,), (0,)))
        return 0

    lax.fori_loop(0, NODES // 512, couple, 0)

    def c_copy(piece, slot, device):
        return pltpu.make_async_remote_copy(
            src_ref=c_send.at[piece],
            dst_ref=c_recv.at[slot],
            send_sem=c_ss.at[piece],
            recv_sem=c_rs.at[slot],
            device_id=device,
            device_id_type=MESH,
        )

    for b in range(BAND):
        block = c_acc[OWN * b : OWN * b + OWN, :]
        turned = jnp.concatenate([block, block], axis=0).T
        for h in range(2):
            piece = 2 * b + h
            upper = turned[32 * h : 32 * h + 16, :]
            lower = turned[32 * h + 16 : 32 * h + 32, :]
            c_send[piece] = jnp.where(low_half[0:16, :], upper, lower)
            to_self = jnp.logical_and(band == b, dom == 2 * band + h)

            @pl.when(jnp.logical_not(to_self))
            def _(b=b, h=h, piece=piece):
                c_copy(piece, dom, {"band": b, "dom": 2 * band + h}).start()

            @pl.when(to_self)
            def _(piece=piece):
                c_recv[dom] = c_send[piece]

    def deliver(group, _):
        for u in range(4):
            j = 4 * group + u
            pot_out[:, tile(j)] = rhs[tile(j), :].T[0:OWN, :]
        return 0

    lax.fori_loop(0, TILES // 4, deliver, 0)

    for off in range(DOM):
        source = lax.rem(dom + off, DOM)
        from_self = jnp.logical_and(mine, source == dom)

        @pl.when(jnp.logical_not(from_self))
        def _(source=source):
            c_copy(0, source, {"band": half_dom, "dom": source}).wait_recv()

    total = jnp.sum(c_recv[...], axis=0) * (1.0 / (NODES * DOM))
    coup_out[...] = jnp.concatenate([total, swap(total)], axis=0)[:, 0:OWN]

    for b in range(BAND):
        for h in range(2):
            piece = 2 * b + h
            to_self = jnp.logical_and(band == b, dom == 2 * band + h)

            @pl.when(jnp.logical_not(to_self))
            def _(b=b, h=h, piece=piece):
                c_copy(piece, dom, {"band": b, "dom": 2 * band + h}).wait_send()


def on_device(
    occ_orb, vir_orb, pair_list, quad_weight, cell_coef, connect, face_map, element_matrix
):
    index = build_index(connect, face_map, occ_orb, vir_orb)
    node, ordered, perm, walk, new, old, orbs = index
    quad = quad_weight.reshape(TILES, 128)
    vmem = pl.BlockSpec(memory_space=pltpu.VMEM)
    smem = pl.BlockSpec(memory_space=pltpu.SMEM)
    dma = pltpu.SemaphoreType.DMA
    field = pltpu.VMEM((NODES, 128), F32)
    potential, coupling = pl.pallas_call(
        main_kernel,
        out_shape=(
            jax.ShapeDtypeStruct((OWN, NODES), F32),
            jax.ShapeDtypeStruct((32, OWN), F32),
        ),
        in_specs=[smem] * 2 + [vmem] * 9,
        out_specs=(vmem, vmem),
        scratch_shapes=[
            pltpu.VMEM((64 * TILES, 128), F32),
            pltpu.VMEM((64, 384), BF16),
            pltpu.VMEM((PAIRS, 64), BF16),
            pltpu.VMEM((PAIRS, 64), BF16),
            pltpu.VMEM((256, 256), BF16),
            field, field, field, field, field, field,
            pltpu.VMEM((CELLS * 128, 128), F32),
            pltpu.VMEM((256, 128), F32),
            pltpu.VMEM((2 * WINDOW - 1, 64, 128), F32),
            pltpu.VMEM((ENTRY_TILES, WINDOW, 64, 128), F32),
            pltpu.VMEM((64 * WINDOW, 128), F32),
            pltpu.VMEM((128, 256), F32),
            pltpu.VMEM((128, 256), F32),
            pltpu.VMEM((PAIRS, NODES), BF16),
            pltpu.VMEM((512, 128), F32),
            pltpu.VMEM((2 * FACE, 128), F32),
            pltpu.VMEM((PAIRS, 128), F32),
            pltpu.VMEM((CELLS, 128), I32),
            pltpu.SMEM((8, 128), I32),
            pltpu.SMEM((8, 128), I32),
            pltpu.VMEM((3, 2, FACE, 128), BF16),
            pltpu.VMEM((3, 2, FACE, 128), BF16),
            pltpu.VMEM((4, 8, 128), F32),
            pltpu.VMEM((4, DOM, 8, 128), F32),
            pltpu.VMEM((DOM, 16, 128), F32),
            pltpu.VMEM((DOM, 16, 128), F32),
            dma((3, 2)),
            dma((3, 2)),
            dma((4, DOM)),
            dma((4, DOM)),
            dma((DOM,)),
            dma((DOM,)),
            dma((2,)),
        ],
        compiler_params=pltpu.CompilerParams(
            collective_id=0, has_side_effects=True, vmem_limit_bytes=60 * 1024 * 1024
        ),
        name="solve",
    )(walk, cell_coef, new, old, node, perm, ordered, orbs, quad, pair_list, element_matrix)
    return potential, coupling.T


def solution(mesh):
    return jax.shard_map(
        on_device,
        mesh=mesh,
        in_specs=(
            P("band", "dom"),
            P("band", "dom"),
            P(),
            P("dom"),
            P("dom"),
            P(None, "dom"),
            P(None, "dom"),
            P(),
        ),
        out_specs=(P("band", "dom"), P("band", "dom")),
        check_vma=False,
    )
```
